32 devices in a mesh: win: 8 (over z, y), tmpl: 4 (over x, core).
Axes of the slice: x: 2, y: 2, z: 4, core: 2. Of those that a mesh axis runs over, the one named last changes fastest.
Arguments:
- raw: bfloat16 [512, 16384], P(('win', 'tmpl')), may hold values from -160 to 160
- ids: int32 [512], replicated, may hold values from -1 to 303, as said below
- fir: bfloat16 [64], replicated, may hold values from -0.75 to 0.75
- taps: bfloat16 [512, 30, 400], P('tmpl'), may hold values from -0.3125 to 0.3125
- channels: int32 [512, 30], P('tmpl'), may hold values from 0 to 303, all different within a row
- shifts: int32 [512, 30], P('tmpl'), may hold values from 0 to 255
Outputs:
- stack: float32 [512, 8192], P('tmpl', 'win')
The draws below stay inside these ranges and needn't reach their ends.
Inputs may be any that keep to these rules, and one draw needn't show every extreme that they name: `ids`: each station channel 0 to 303 stands in exactly one slot, the others hold -1; the owners of one index of tmpl hold exactly 76 live slots together, and one owner of each holds 16 live slots. Each template names 30 different channels; every channel is named by some template.
All inputs are finite; a program needn't handle non-finite values.
Results may differ from the reference program's by a relative error of at most 0.007.
Values may be sent and summed in bfloat16 or wider, within the bound.
No kernel may reach another device: no remote copies, remote signals or barrier semaphores. Data moves between devices by JAX's collectives and lax.ppermute only.
A program may use at most 128 MiB of HBM per device.

```python
import math
import jax
import jax.numpy as jnp
from jax import lax

WIN_DEV = 1024
MARGIN = 768
TL = 400
CH = 30
DEC = 2
NTAP = 64
MOVE = 256
SLOTS = 16
NS = 1792
NF = 896
NCHAN = 304
ROWS_ALL = 512
RAW_T = 16384
TEMPLATES = 512
TIMES = 8192
N_WIN = 8
N_TMPL = 4


def draw_raw(key, part):
    noise_key, row_key, envelope_key = jax.random.split(key, 3)
    base = jnp.clip(jax.random.normal(noise_key, (ROWS_ALL, RAW_T), jnp.float32), -4.0, 4.0)
    row_scale = jnp.exp(jax.random.uniform(row_key, (ROWS_ALL, 1), jnp.float32, 0.0, math.log(10.0)))
    envelope = jnp.exp(jax.random.uniform(envelope_key, (ROWS_ALL, RAW_T // 64, 1), jnp.float32, 0.0, math.log(4.0)))
    shaped = (base.reshape(ROWS_ALL, RAW_T // 64, 64) * envelope).reshape(ROWS_ALL, RAW_T)
    return (shaped * row_scale).astype(jnp.bfloat16)


def draw_ids(key, part):
    column_count = N_WIN * SLOTS
    live_col = 3 * SLOTS * N_WIN // 5

    def column(subkey):
        owner_key, rank_key = jax.random.split(subkey)
        owner = jax.random.randint(owner_key, (), 0, N_WIN)
        slot_owner = jnp.arange(column_count, dtype=jnp.int32) // SLOTS
        ranking = jax.random.permutation(rank_key, column_count).astype(jnp.int32)
        score = jnp.where(slot_owner == owner, -1, ranking)
        ordering = jnp.argsort(score, stable=True)
        placing = jnp.argsort(ordering)
        return placing < live_col
    column_keys = jax.random.split(jax.random.fold_in(key, 7), N_TMPL)
    live = jax.vmap(column)(column_keys)
    live = live.reshape(N_TMPL, N_WIN, SLOTS).transpose(1, 0, 2).reshape(-1)
    channel_perm = jax.random.permutation(jax.random.fold_in(key, 11), NCHAN).astype(jnp.int32)
    counter = jnp.cumsum(live.astype(jnp.int32)) - 1
    picked = jnp.take(channel_perm, jnp.clip(counter, 0, NCHAN - 1))
    return jnp.where(live, picked, -1).astype(jnp.int32)


def with_ends(entries, rng, least, top_value):
    longest = entries.shape.index(max(entries.shape))
    spots = []
    for shift in (0, 1):
        where = [jax.random.randint(jax.random.fold_in(rng, axis), (), 0, length) for axis, length in enumerate(entries.shape)]
        where[longest] = (where[longest] + shift) % entries.shape[longest]
        spots.append(tuple(where))
    return entries.at[spots[0]].set(least).at[spots[1]].set(top_value)


def level_of(own_key, shape, cuts, smallest, largest):
    factor_of, own = 1.0, jax.random.fold_in(own_key, 6)
    for dim, parts in cuts:
        draws = jnp.exp(jax.random.uniform(jax.random.fold_in(own, dim), (parts,), jnp.float32, smallest / len(cuts), largest / len(cuts)))
        factor_of = factor_of * jnp.repeat(draws, shape[dim] // parts).reshape([-1 if axis == dim else 1 for axis in range(len(shape))])
    return factor_of


def different_ones(own_key, rows, number_of, top, lift):
    sequence = jax.random.permutation(jax.random.fold_in(own_key, 1), number_of)
    pull = sequence
    for power in range(3):
        pull = pull * pull // number_of
    pull = pull * lift // number_of
    tickets = jax.random.randint(jax.random.fold_in(own_key, 2), (rows, number_of), 0, 4096) + pull
    sure = jax.random.permutation(jax.random.fold_in(own_key, 3), rows)[jnp.arange(number_of) % rows]
    tickets = jnp.where(jnp.arange(rows)[:, None] == sure[None, :], 1 << 14, tickets)
    score = tickets * number_of + jnp.arange(number_of)
    return lax.top_k(score.astype(jnp.int32), top)[1].astype(jnp.int32)


def gaussian(stream_key, dims, scale, limit, cuts=(), kind=jnp.bfloat16):
    drawn = jax.random.normal(stream_key, dims, jnp.float32) * scale
    if len(cuts) > 0:
        drawn = level_of(stream_key, dims, cuts, -0.22, 0.18) * drawn
    return jnp.clip(drawn, min=-limit, max=limit).astype(kind)


def setup_inputs(seed: int = 0) -> dict:
    key_list = jax.random.split(jax.random.key(seed), 7)
    return {
        "raw": draw_raw(jax.random.fold_in(key_list[6], 71), 0),
        "ids": draw_ids(jax.random.fold_in(key_list[6], 71), 0),
        "fir": gaussian(key_list[2], (NTAP,), NTAP ** -0.5, 0.75),
        "taps": gaussian(key_list[3], (TEMPLATES, CH, TL), TL ** -0.5, 0.3125, ((0, 4),)),
        "channels": different_ones(key_list[4], TEMPLATES, NCHAN, CH, 808),
        "shifts": with_ends(jax.random.randint(key_list[5], (TEMPLATES, CH), 0, MOVE), jax.random.fold_in(key_list[5], 1), 0, MOVE - 1).astype(jnp.int32),
    }


def band_matrix(fir, block):
    in_index = jnp.arange(DEC * block + NTAP, dtype=jnp.int32)[:, None]
    out_index = jnp.arange(block, dtype=jnp.int32)[None, :]
    offset = in_index - DEC * out_index
    onehot = offset[:, :, None] == jnp.arange(NTAP, dtype=jnp.int32)[None, None, :]
    values = jnp.where(onehot, fir.astype(jnp.float32)[None, None, :], jnp.float32(0.0))
    return lax.optimization_barrier(jnp.sum(values, axis=2)).astype(jnp.bfloat16)

def decimate(raw_ext, fir, count):
    block = math.gcd(count, 128)
    pieces = count // block
    length = DEC * block
    height = raw_ext.shape[0]
    padded = jnp.pad(raw_ext, ((0, 0), (0, (pieces + 1) * length - raw_ext.shape[1])))
    blocks = padded.reshape(height, pieces + 1, length)
    segments = jnp.concatenate([blocks[:, :pieces], blocks[:, 1:, :NTAP]], axis=2)
    band = band_matrix(fir, block)
    result = jnp.einsum('rbi,in->rbn', segments, band, preferred_element_type=jnp.float32)
    return result.reshape(height, count)

def forward_table():
    sample_index = jnp.arange(NS, dtype=jnp.int32)[:, None]
    frequency = jnp.arange(NF, dtype=jnp.int32)[None, :]
    angle = (sample_index * frequency % NS).astype(jnp.float32) * jnp.float32(2.0 * math.pi / NS)
    return jnp.concatenate([jnp.cos(angle), jnp.sin(angle)], axis=1).astype(jnp.bfloat16)

def inverse_table():
    frequency = jnp.arange(NF, dtype=jnp.int32)[:, None]
    time_index = jnp.arange(WIN_DEV, dtype=jnp.int32)[None, :]
    angle = (frequency * time_index % NS).astype(jnp.float32) * jnp.float32(2.0 * math.pi / NS)
    return jnp.concatenate([jnp.cos(angle), -jnp.sin(angle)], axis=0).astype(jnp.bfloat16)

def spectra(tiles, table):
    values = tiles.astype(jnp.float32)
    scale = lax.rsqrt(lax.optimization_barrier(jnp.mean(values * values, axis=1, keepdims=True)) + 1e-05)
    return (jnp.dot(tiles, table, preferred_element_type=jnp.float32) * scale).astype(jnp.bfloat16)

def stack_block(template_spec, data_spec, shift_block, inverse):
    tmpl_cos = template_spec[:, :NF].astype(jnp.float32)
    tmpl_sin = template_spec[:, NF:].astype(jnp.float32)
    data_cos = data_spec[:, :NF].astype(jnp.float32)
    data_sin = data_spec[:, NF:].astype(jnp.float32)
    real_part = tmpl_cos * data_cos + tmpl_sin * data_sin
    imag_part = tmpl_sin * data_cos - tmpl_cos * data_sin
    frequency = jnp.arange(NF, dtype=jnp.int32)[None, :]
    angle = (shift_block[:, None] * frequency % NS).astype(jnp.float32) * jnp.float32(2.0 * math.pi / NS)
    phase_cos = jnp.cos(angle)
    phase_sin = jnp.sin(angle)
    rotated_real = real_part * phase_cos - imag_part * phase_sin
    rotated_imag = real_part * phase_sin + imag_part * phase_cos
    group = shift_block.shape[0] // CH
    summed_real = lax.optimization_barrier(jnp.sum(rotated_real.reshape(group, CH, NF), axis=1))
    summed_imag = lax.optimization_barrier(jnp.sum(rotated_imag.reshape(group, CH, NF), axis=1))
    weight = jnp.where(jnp.arange(NF) == 0, 1.0, 2.0).astype(jnp.float32) / jnp.float32(CH * NS)
    packed = jnp.concatenate([summed_real * weight, summed_imag * weight], axis=1).astype(jnp.bfloat16)
    return jnp.dot(packed, inverse, preferred_element_type=jnp.float32)

def reference(raw, ids, fir, taps, channels, shifts):
    whole = jnp.pad(raw, ((0, 0), (0, NTAP)))
    filtered = decimate(whole, fir, TIMES).astype(jnp.bfloat16)
    position = jnp.arange(ROWS_ALL, dtype=jnp.int32)
    keyed = jnp.where(ids >= 0, ids, NCHAN + position)
    row_of = jnp.argsort(keyed)[:NCHAN].astype(jnp.int32)
    by_channel = jnp.take(filtered, row_of, axis=0)
    padded = jnp.pad(by_channel, ((0, 0), (0, MARGIN)))
    forward = forward_table()
    inverse = inverse_table()
    template_spec = jnp.dot(taps.reshape(-1, TL), forward[:TL], preferred_element_type=jnp.float32).astype(jnp.bfloat16)
    flat_channels = channels.reshape(-1).astype(jnp.int32)
    flat_shifts = shifts.reshape(-1).astype(jnp.int32)
    group = math.gcd(TEMPLATES, 64)
    count = TEMPLATES // group

    def one_window(window_index):
        tiles = lax.dynamic_slice_in_dim(padded, (window_index * WIN_DEV).astype(jnp.int32), NS, 1)
        spec = spectra(tiles, forward)

        def one_block(block_index):
            begin = (block_index * group * CH).astype(jnp.int32)
            spec_block = lax.dynamic_slice_in_dim(template_spec, begin, group * CH, 0)
            chan_block = lax.dynamic_slice_in_dim(flat_channels, begin, group * CH, 0)
            shift_block = lax.dynamic_slice_in_dim(flat_shifts, begin, group * CH, 0)
            data_spec = jnp.take(spec, chan_block, axis=0)
            return stack_block(spec_block, data_spec, shift_block, inverse)
        return lax.map(one_block, jnp.arange(count, dtype=jnp.int32)).reshape(TEMPLATES, WIN_DEV)
    stacks = lax.map(one_window, jnp.arange(N_WIN, dtype=jnp.int32))
    return jnp.transpose(stacks, (1, 0, 2)).reshape(TEMPLATES, TIMES)
```

```python
import functools
import math

import jax
import jax.numpy as jnp
import ml_dtypes
import numpy as np
from jax import lax
from jax.experimental import pallas as pl
from jax.experimental.pallas import tpu as pltpu
from jax.sharding import PartitionSpec as P

WIN_DEV = 1024
TL = 400
CH = 30
DEC = 2
NTAP = 64
MOVE = 256
NS = 1792
NF = 896
LANE = 128
TILES = NF // LANE
BLOCK = 128
SPAN = 384
MIB = 2**20
BF16 = jnp.bfloat16
F32 = jnp.float32


def angles(rows, columns):
    step = np.float32(2.0 * math.pi / NS)
    turns = np.arange(rows)[:, None] * np.arange(columns)[None, :] % NS
    return (turns.astype(np.float32) * step).astype(np.float64)


def forward_table():
    angle = angles(NS, NF)
    return np.concatenate([np.cos(angle), np.sin(angle)], axis=1).astype(ml_dtypes.bfloat16)


def inverse_table():
    angle = angles(NF, WIN_DEV)
    return np.concatenate([np.cos(angle), -np.sin(angle)], axis=0).astype(ml_dtypes.bfloat16)


def phase_table():
    angle = angles(MOVE, NF)
    slab = np.zeros((MOVE, 16, LANE), np.float32)
    slab[:, :TILES] = np.cos(angle).reshape(MOVE, TILES, LANE)
    slab[:, 8 : 8 + TILES] = np.sin(angle).reshape(MOVE, TILES, LANE)
    return slab


def spectra_kernel(win_ref, raw_ref, fir_ref, table_hbm, *rest):
    win_count = (len(rest) - 4) if len(rest) > 4 else 0
    outs = rest[:win_count]
    table, filt, tile, sem = rest[win_count:]
    slots, raw_t = raw_ref.shape
    blocks = raw_t // (DEC * BLOCK)
    load = pltpu.make_async_copy(table_hbm, table, sem)
    load.start()
    spread = jnp.broadcast_to(fir_ref[...], (BLOCK, SPAN))
    band = pltpu.roll(spread, 0, 1, stride=DEC, stride_axis=0).astype(BF16)
    pieces = []
    for b in range(blocks):
        begin = b * DEC * BLOCK
        if begin + SPAN <= raw_t:
            pieces.append(raw_ref[:, begin : begin + SPAN])
        else:
            pad = jnp.zeros((slots, begin + SPAN - raw_t), BF16)
            pieces.append(jnp.concatenate([raw_ref[:, begin:raw_t], pad], axis=1))
    segments = jnp.concatenate(pieces, axis=0)
    result = lax.dot_general(segments, band, (((1,), (1,)), ((), ())), preferred_element_type=F32)
    filt[0 : blocks * slots] = result.astype(BF16)
    per_win = WIN_DEV // BLOCK
    per_tile = NS // BLOCK
    extra = per_tile - per_win
    filt[blocks * slots :] = jnp.zeros((extra * slots, BLOCK), BF16)
    for d in range(win_count):
        first = (win_ref[0] ^ d) * per_win
        for m in range(per_tile):
            start = pl.multiple_of((first + m) * slots, slots)
            tile[d * slots : (d + 1) * slots, m * BLOCK : (m + 1) * BLOCK] = filt[pl.ds(start, slots), :]
    values = tile[...].astype(F32)
    scale = lax.rsqrt(jnp.mean(values * values, axis=1, keepdims=True) + 1e-05)
    load.wait()
    spec = jnp.dot(tile[...], table[...], preferred_element_type=F32) * scale
    spec = spec.astype(BF16)
    for d in range(win_count):
        outs[d][...] = spec[d * slots : (d + 1) * slots]


def compact_kernel(ids_ref, *rest):
    blocks, out_ref = rest[:-1], rest[-1]
    rows = out_ref.shape[0]
    count = ids_ref.shape[1]
    live = ids_ref[...] >= 0
    above = lax.broadcasted_iota(jnp.int32, (count, count), 0) < lax.broadcasted_iota(
        jnp.int32, (count, count), 1
    )
    marks = jnp.broadcast_to(jnp.where(live, 1.0, 0.0), (16, count)).astype(BF16)
    rank = jnp.dot(marks, jnp.where(above, 1.0, 0.0).astype(BF16), preferred_element_type=F32)
    rank = jnp.where(live, rank[0:1], -1.0)
    wanted = lax.broadcasted_iota(jnp.int32, (rows, count), 0).astype(F32)
    pick = jnp.where(wanted == rank, 1.0, 0.0).astype(BF16)
    data = jnp.concatenate([block[...] for block in blocks], axis=0)
    out_ref[...] = jnp.dot(pick, data, preferred_element_type=F32).astype(BF16)


def template_kernel(sizes, shift_ref, ids_ref, place_ref, taps_ref, table_ref, phase_ref, u_ref, label_ref, flat):
    templates = taps_ref.shape[2]
    win_count, tmpl_count, slots, rows = sizes

    def channel(j, carry):
        wave = jnp.transpose(taps_ref[j])
        for m in range(TILES):
            part = jnp.dot(wave, table_ref[:, 2 * m * LANE : 2 * (m + 1) * LANE], preferred_element_type=F32)
            for g in range(templates // 8):
                for h in range(2):
                    at = (g * 2 * TILES + 2 * m + h) * 8
                    flat[at : at + 8, :] = part[g * 8 : (g + 1) * 8, h * LANE : (h + 1) * LANE]

        def eight(g, inner):
            for r in range(8):
                k = g * 8 + r
                at = g * (2 * TILES * 8) + r
                t_cos = flat[pl.ds(at, 8, stride=8), :]
                t_sin = flat[pl.ds(at + TILES * 8, 8, stride=8), :]
                shift = shift_ref[j, k]
                p_cos = phase_ref[shift, 0:8]
                p_sin = phase_ref[shift, 8:16]
                u_ref[k * CH + j, 0:8] = (t_cos * p_cos - t_sin * p_sin).astype(u_ref.dtype)
                u_ref[k * CH + j, 8:16] = (t_sin * p_cos + t_cos * p_sin).astype(u_ref.dtype)
            return inner

        return lax.fori_loop(0, templates // 8, eight, carry)

    lax.fori_loop(0, CH, channel, 0)

    def column(d, carry):
        def slot(q, count):
            owner = place_ref[0] ^ (q // slots)
            at = (owner * tmpl_count + (place_ref[1] ^ d)) * slots + q % slots
            label = ids_ref[at]
            label_ref[d * rows + jnp.minimum(count, rows - 1)] = label
            return count + (label >= 0).astype(jnp.int32)

        lax.fori_loop(0, win_count * slots, slot, 0)
        return carry

    lax.fori_loop(0, tmpl_count, column, 0)


def stack_kernel(live, chan_ref, label_ref, u_ref, inverse_hbm, *rest):
    pieces, (out_ref, inverse, flat, slabs, z, packed, sem) = rest[:-7], rest[-7:]
    templates = out_ref.shape[0]
    load = pltpu.make_async_copy(inverse_hbm, inverse, sem)
    load.start()
    rows = pieces[0].shape[0]
    for d, piece in enumerate(pieces):
        for g in range(rows // 16):
            for m in range(2 * TILES):
                value = piece[g * 16 : (g + 1) * 16, m * LANE : (m + 1) * LANE].astype(F32)
                for h in range(2):
                    at = ((2 * g + h) * 2 * TILES + m) * 8
                    flat[at : at + 8, :] = value[h * 8 : (h + 1) * 8]
        for r in range(live):
            at = (r // 8) * (2 * TILES * 8) + r % 8
            label = label_ref[d * rows + r]
            slabs[label, 0:8] = flat[pl.ds(at, 8, stride=8), :]
            slabs[label, 8:16] = flat[pl.ds(at + TILES * 8, 8, stride=8), :]

    step = 8

    def some(i, carry):
        for q in range(step):
            k = i * step + q
            real, imag = [None, None], [None, None]
            for j in range(CH):
                c = chan_ref[i * (step * 32) + (q * 32 + j)]
                u_cos = u_ref[k * CH + j, 0:8].astype(F32)
                u_sin = u_ref[k * CH + j, 8:16].astype(F32)
                x_cos = slabs[c, 0:8]
                x_sin = slabs[c, 8:16]
                re = u_cos * x_cos + u_sin * x_sin
                im = u_sin * x_cos - u_cos * x_sin
                p = j % 2
                real[p] = re if real[p] is None else real[p] + re
                imag[p] = im if imag[p] is None else imag[p] + im
            at = pl.multiple_of(k * 16, 16)
            z[pl.ds(at, 8), :] = real[0] + real[1]
            z[pl.ds(at + 8, 8), :] = imag[0] + imag[1]
        return carry

    lax.fori_loop(0, templates // step, some, 0)
    first = lax.broadcasted_iota(jnp.int32, (16, LANE), 1) == 0
    base = jnp.float32(CH * NS)
    for m in range(2 * TILES):
        row = m if m < TILES else m - TILES + 8
        weight = jnp.float32(2.0) / base
        if m % TILES == 0:
            weight = jnp.where(first, jnp.float32(1.0), jnp.float32(2.0)) / base
        for g in range(templates // 16):
            low = z[pl.ds(g * 256 + row, 8, stride=16), :]
            high = z[pl.ds(g * 256 + 128 + row, 8, stride=16), :]
            value = jnp.concatenate([low, high], axis=0) * weight
            packed[g * 16 : (g + 1) * 16, m * LANE : (m + 1) * LANE] = value.astype(BF16)
    load.wait()
    out_ref[...] = jnp.dot(packed[...], inverse[...], preferred_element_type=F32)


def full(space=pltpu.VMEM):
    return pl.BlockSpec(memory_space=space)


def on_device(raw, ids, fir, taps, channels, shifts):
    win_count = lax.axis_size("win")
    tmpl_count = lax.axis_size("tmpl")
    win = lax.axis_index("win")
    tmpl = lax.axis_index("tmpl")
    slots, raw_t = raw.shape
    templates = taps.shape[0]
    live = 3 * slots * win_count // 5
    rows = -(-live // 16) * 16
    chan_total = live * tmpl_count
    table = jnp.asarray(forward_table())
    inverse = jnp.asarray(inverse_table())
    phase = jnp.asarray(phase_table())

    blocks = raw_t // (DEC * BLOCK)
    fir_row = jnp.pad(fir.astype(F32), (0, SPAN - NTAP))[None, :]
    extra = (NS - WIN_DEV) // BLOCK
    mine = pl.pallas_call(
        spectra_kernel,
        out_shape=[jax.ShapeDtypeStruct((slots, NS), BF16)] * win_count,
        in_specs=[full(pltpu.SMEM), full(), full(), full(pl.ANY)],
        out_specs=[full()] * win_count,
        scratch_shapes=[
            pltpu.VMEM((NS, 2 * NF), BF16),
            pltpu.VMEM(((blocks + extra) * slots, BLOCK), BF16),
            pltpu.VMEM((win_count * slots, NS), BF16),
            pltpu.SemaphoreType.DMA,
        ],
        compiler_params=pltpu.CompilerParams(vmem_limit_bytes=20 * MIB),
        name="spectra",
    )(win.reshape(1), raw, fir_row, table)

    parts = [mine[0]]
    for d in range(1, win_count):
        parts.append(lax.ppermute(mine[d], "win", [(i, i ^ d) for i in range(win_count)]))

    grid = ids.reshape(win_count, tmpl_count, slots)
    owners = win ^ jnp.arange(win_count, dtype=jnp.int32)
    column = jnp.take(lax.dynamic_index_in_dim(grid, tmpl, 1, keepdims=False), owners, axis=0)
    packed_rows = pl.pallas_call(
        compact_kernel,
        out_shape=jax.ShapeDtypeStruct((rows, NS), BF16),
        in_specs=[full()] * (1 + win_count),
        out_specs=full(),
        compiler_params=pltpu.CompilerParams(vmem_limit_bytes=20 * MIB),
        name="compact",
    )(column.reshape(1, win_count * slots), *parts)

    held = {0: packed_rows}
    bit = tmpl_count // 2
    while bit:
        for d in list(held):
            held[d | bit] = lax.ppermute(held[d], "tmpl", [(i, i ^ bit) for i in range(tmpl_count)])
        bit //= 2
    pieces = [held[d] for d in range(tmpl_count)]

    slab_type = F32 if chan_total <= 1024 else BF16
    sizes = (win_count, tmpl_count, slots, rows)
    place = jnp.stack([win, tmpl]).astype(jnp.int32)
    slabs, labels = pl.pallas_call(
        functools.partial(template_kernel, sizes),
        out_shape=[
            pltpu.VMEM((templates * CH, 16, LANE), slab_type),
            jax.ShapeDtypeStruct((tmpl_count * rows,), jnp.int32),
        ],
        in_specs=[full(pltpu.SMEM)] * 3 + [full()] * 3,
        out_specs=[full(), full(pltpu.SMEM)],
        scratch_shapes=[pltpu.VMEM((templates // 8 * 2 * TILES * 8 + 64, LANE), F32)],
        compiler_params=pltpu.CompilerParams(vmem_limit_bytes=16 * MIB),
        name="templates",
    )(shifts.T, ids, place, taps.transpose(1, 2, 0), table[:TL], phase)

    slabs = pltpu.with_memory_space_constraint(slabs, pltpu.VMEM)
    chan = jnp.pad(channels, ((0, 0), (0, 32 - CH))).reshape(-1)
    return pl.pallas_call(
        functools.partial(stack_kernel, live),
        out_shape=jax.ShapeDtypeStruct((templates, WIN_DEV), F32),
        in_specs=[full(pltpu.SMEM)] * 2 + [full(), full(pl.ANY)] + [full()] * tmpl_count,
        out_specs=full(),
        scratch_shapes=[
            pltpu.VMEM((2 * NF, WIN_DEV), BF16),
            pltpu.VMEM((rows * 2 * TILES + 64, LANE), F32),
            pltpu.VMEM((chan_total, 16, LANE), F32),
            pltpu.VMEM((templates * 16, LANE), F32),
            pltpu.VMEM((templates, NS), BF16),
            pltpu.SemaphoreType.DMA,
        ],
        compiler_params=pltpu.CompilerParams(vmem_limit_bytes=(20 if slab_type == F32 else 42) * MIB),
        name="stacks",
    )(chan, labels, slabs, inverse, *pieces)


def solution(mesh):
    return jax.shard_map(
        on_device,
        mesh=mesh,
        in_specs=(
            P(("win", "tmpl"), None),
            P(),
            P(),
            P("tmpl", None, None),
            P("tmpl", None),
            P("tmpl", None),
        ),
        out_specs=P("tmpl", "win"),
        check_vma=False,
    )
```

```python
import functools
import math

import jax
import jax.numpy as jnp
import ml_dtypes
import numpy as np
from jax import lax
from jax.experimental import pallas as pl
from jax.experimental.pallas import tpu as pltpu
from jax.sharding import PartitionSpec as P

WIN_DEV = 1024
TL = 400
CH = 30
DEC = 2
NTAP = 64
MOVE = 256
NS = 1792
NF = 896
LANE = 128
TILES = NF // LANE
BLOCK = 256
SPAN = 640
PITCH = 2 * TILES
MIB = 2**20
BF16 = jnp.bfloat16
F32 = jnp.float32


def angles(rows, columns):
    step = np.float32(2.0 * math.pi / NS)
    turns = np.arange(rows)[:, None] * np.arange(columns)[None, :] % NS
    return (turns.astype(np.float32) * step).astype(np.float64)


def order():
    low = np.arange(3 * LANE)
    high = NF - low
    high[0] = NF // 2
    rest = np.arange(3 * LANE, NF // 2)
    return np.concatenate([low, high, rest, NF - rest])


def forward_tables():
    angle = angles(NS, NF)
    cosine, sine = np.cos(angle), np.sin(angle)
    full = 3 * LANE
    half = NF // 2
    columns = [cosine[:, :full], sine[:, :full], cosine[:, full:half], sine[:, full:half]]
    table = np.concatenate(columns, axis=1)
    even, odd = table[0::2].copy(), table[1::2].copy()
    even[:, full] = cosine[0::2, half]
    odd[:, full] = sine[1::2, half]
    return np.stack([even, odd]).astype(ml_dtypes.bfloat16)


def inverse_table():
    angle = angles(NF, WIN_DEV)[order()]
    return np.concatenate([np.cos(angle), -np.sin(angle)], axis=0).astype(ml_dtypes.bfloat16)


def phase_table():
    angle = angles(MOVE, NF)[:, order()]
    slab = np.zeros((MOVE, 16, LANE), np.float32)
    slab[:, :TILES] = np.cos(angle).reshape(MOVE, TILES, LANE)
    slab[:, 8 : 8 + TILES] = np.sin(angle).reshape(MOVE, TILES, LANE)
    return slab


def tile_of(array, column):
    return array[:, column * LANE : (column + 1) * LANE]


def butterfly(even, odd):
    low = [tile_of(even, c) + tile_of(odd, c) for c in range(TILES)]
    lane = lax.broadcasted_iota(jnp.int32, low[0].shape, 1)
    first, left = lane == 0, lane < LANE // 2
    high_cos = [tile_of(even, c) - tile_of(odd, c) for c in range(3)]
    high_sin = [tile_of(odd, 3 + c) - tile_of(even, 3 + c) for c in range(3)]
    high_cos[0] = jnp.where(first, tile_of(even, 3), high_cos[0])
    high_sin[0] = jnp.where(first, tile_of(odd, 3), high_sin[0])
    low_sin = low[3:6]
    low_sin[0] = jnp.where(first, 0.0, low_sin[0])
    gap = tile_of(even, 6) - tile_of(odd, 6)
    mixed_cos = jnp.where(left, low[6], pltpu.roll(gap, LANE // 2, 1))
    mixed_sin = jnp.where(left, pltpu.roll(low[6], LANE // 2, 1), -gap)
    return low[0:3] + high_cos + [mixed_cos] + low_sin + high_sin + [mixed_sin]


def spectra_kernel(place_ref, raw_hbm, fir_hbm, table_hbm, *rest):
    win_count = len(rest) - 6
    outs = rest[:win_count]
    raw, fir, table, filt, tile, sems = rest[win_count:]
    slots, raw_t = raw_hbm.shape
    length = DEC * BLOCK
    blocks = raw_t // length
    raw_copy = pltpu.make_async_copy(raw_hbm, raw.at[:, 0:raw_t], sems.at[0])
    raw_copy.start()
    fir_copy = pltpu.make_async_copy(fir_hbm, fir, sems.at[1])
    fir_copy.start()
    loads = [pltpu.make_async_copy(table_hbm.at[p], table.at[p], sems.at[2 + p]) for p in range(2)]
    for load in loads:
        load.start()
    raw[:, raw_t:] = jnp.zeros((slots, SPAN - length), BF16)
    fir_copy.wait()
    taps = jnp.concatenate([fir[...].astype(F32), jnp.zeros((1, SPAN - NTAP), F32)], axis=1)
    spread = jnp.broadcast_to(taps, (BLOCK // 2, SPAN))
    even = pltpu.roll(spread, 0, 1, stride=2 * DEC, stride_axis=0)
    odd = pltpu.roll(spread, DEC, 1, stride=2 * DEC, stride_axis=0)
    band = jnp.concatenate([even, odd], axis=0).astype(BF16)
    raw_copy.wait()
    segments = jnp.concatenate([raw[:, b * length : b * length + SPAN] for b in range(blocks)], axis=0)
    result = lax.dot_general(segments, band, (((1,), (1,)), ((), ())), preferred_element_type=F32)
    filt[0 : blocks * slots] = result.astype(BF16)
    per_win = WIN_DEV // BLOCK
    per_tile = NS // BLOCK
    filt[blocks * slots :] = jnp.zeros(((per_tile - per_win) * slots, BLOCK), BF16)
    for d in range(win_count):
        first = (place_ref[0] ^ d) * per_win
        for m in range(per_tile):
            start = pl.multiple_of((first + m) * slots, slots)
            block = filt[pl.ds(start, slots), :]
            for p in range(2):
                tile[p, d * slots : (d + 1) * slots, m * LANE : (m + 1) * LANE] = tile_of(block, p)
    values = tile[...].astype(F32)
    scale = lax.rsqrt(jnp.sum(jnp.sum(values * values, axis=2, keepdims=True), axis=0) / NS + 1e-05)
    sums = []
    for p in range(2):
        loads[p].wait()
        sums.append(jnp.dot(tile[p], table[p], preferred_element_type=F32))
    for column, value in enumerate(butterfly(*sums)):
        value = (value * scale).astype(BF16)
        for d in range(win_count):
            outs[d][:, column * LANE : (column + 1) * LANE] = value[d * slots : (d + 1) * slots]


def column_ids(ids, tmpl, tmpl_count, slots):
    total = ids.shape[1]
    count = total // tmpl_count
    source = lax.broadcasted_iota(jnp.int32, (total, count), 0)
    target = lax.broadcasted_iota(jnp.int32, (total, count), 1)
    wanted = (target // slots * tmpl_count + tmpl) * slots + target % slots
    pick = jnp.where(source == wanted, 1.0, 0.0).astype(BF16)
    digits = jnp.concatenate([(ids + 1) // 64, (ids + 1) % 64], axis=0).astype(F32)
    digits = jnp.concatenate([digits, jnp.zeros((14, total), F32)], axis=0).astype(BF16)
    found = jnp.dot(digits, pick, preferred_element_type=F32)
    return found[0:1], found[1:2]


def picks(high, low, rows):
    count = high.shape[1]
    live = high + low > 0.0
    above = lax.broadcasted_iota(jnp.int32, (count, count), 0) < lax.broadcasted_iota(
        jnp.int32, (count, count), 1
    )
    marks = jnp.broadcast_to(jnp.where(live, 1.0, 0.0), (16, count)).astype(BF16)
    rank = jnp.dot(marks, jnp.where(above, 1.0, 0.0).astype(BF16), preferred_element_type=F32)
    rank = jnp.where(live, rank[0:1], -1.0)
    wanted = lax.broadcasted_iota(jnp.int32, (rows, count), 0).astype(F32)
    return jnp.where(wanted == rank, 1.0, 0.0).astype(BF16)


def compact_kernel(tmpl_count, place_ref, ids_ref, *rest):
    blocks, out_ref, data = rest[:-2], rest[-2], rest[-1]
    slots = blocks[0].shape[0]
    high, low = column_ids(ids_ref[...], place_ref[1], tmpl_count, slots)
    pick = picks(high, low, out_ref.shape[0])
    for d, block in enumerate(blocks):
        start = pl.multiple_of((place_ref[0] ^ d) * slots, slots)
        data[pl.ds(start, slots), :] = block[...]
    out_ref[...] = jnp.dot(pick, data[...], preferred_element_type=F32).astype(BF16)


def template_kernel(slots, shift_ref, after_ref, ids_ref, taps_ref, table_ref, phase_ref, *rest):
    u_ref, label_ref, flat_a, flat_b, wave = rest
    templates = taps_ref.shape[2]
    group = u_ref.shape[1] // 2
    groups = CH // group
    step = pl.program_id(0)

    def transform(index, flat):
        halves = [[], []]
        for j in range(group):
            wave[...] = taps_ref[index * group + j].astype(F32)
            for p in range(2):
                halves[p].append(jnp.transpose(wave[pl.ds(p, TL // 2, stride=2), :]).astype(BF16))
        sums = [
            jnp.dot(jnp.concatenate(halves[p], axis=0), table_ref[p], preferred_element_type=F32) for p in range(2)
        ]
        for column, value in enumerate(butterfly(*sums)):
            for g in range(group * templates // 8):
                flat[pl.ds(g * 8 * PITCH + column, 8, stride=PITCH), :] = value[g * 8 : (g + 1) * 8]

    def turn(index, flat, half):
        for k in range(templates):
            for j in range(group):
                at = (j * templates + k) * PITCH
                t_cos = flat[at : at + 8, :]
                t_sin = flat[at + TILES : at + TILES + 8, :]
                shift = shift_ref[index * group + j, k]
                p_cos = phase_ref[shift, 0:8]
                p_sin = phase_ref[shift, 8:16]
                real = t_cos * p_cos - t_sin * p_sin
                imag = t_sin * p_cos + t_cos * p_sin
                u_ref[k, half * group + j] = jnp.concatenate([real, imag], axis=0).astype(BF16)

    @pl.when(step == 0)
    def _():
        flat_a[group * templates * PITCH :, :] = jnp.zeros((8, LANE), F32)
        flat_b[group * templates * PITCH :, :] = jnp.zeros((8, LANE), F32)
        transform(0, flat_a)
        tmpl_count, width = label_ref.shape
        for t in range(tmpl_count):
            high, low = column_ids(ids_ref[...], t, tmpl_count, slots)
            digits = jnp.concatenate([high, low, jnp.zeros((14, high.shape[1]), F32)], axis=0).astype(BF16)
            pick = picks(high, low, width)
            row = lax.dot_general(digits, pick, (((1,), (1,)), ((), ())), preferred_element_type=F32)
            label_ref[t : t + 1, :] = (row[0:1] * 64.0 + row[1:2]).astype(jnp.int32) - 1

    transform(2 * step + 1, flat_b)
    turn(2 * step, flat_a, 0)
    transform(jnp.minimum(2 * step + 2, groups - 1), flat_a)
    turn(2 * step + 1, flat_b, 1)


def stack_kernel(live, place_ref, chan_ref, label_ref, u_hbm, inverse_hbm, *rest):
    pieces = rest[:-8]
    out_ref, u_all, inverse, flat, slabs, z, packed, sems = rest[-8:]
    templates = out_ref.shape[0]
    parts = 8
    some = templates // parts
    loads = []
    for i in range(parts):
        part = slice(i * some, (i + 1) * some)
        loads.append(pltpu.make_async_copy(u_hbm.at[part], u_all.at[part], sems.at[i]))
        loads[-1].start()
    table_copy = pltpu.make_async_copy(inverse_hbm, inverse, sems.at[parts])
    table_copy.start()
    rows = pieces[0].shape[0]
    tmpl = place_ref[1]
    flat[rows * PITCH :, :] = jnp.zeros((8, LANE), F32)
    for d, piece in enumerate(pieces):
        for g in range(rows // 16):
            for column in range(2 * TILES):
                value = piece[g * 16 : (g + 1) * 16, column * LANE : (column + 1) * LANE].astype(F32)
                for h in range(2):
                    flat[pl.ds((2 * g + h) * 8 * PITCH + column, 8, stride=PITCH), :] = value[h * 8 : (h + 1) * 8]
        for r in range(live):
            label = label_ref[tmpl ^ d, r]
            slabs[label, 0:8] = flat[r * PITCH : r * PITCH + 8]
            slabs[label, 8:16] = flat[r * PITCH + TILES : r * PITCH + TILES + 8]

    step = 4

    def several(i, carry):
        for q in range(step):
            k = i * step + q
            real, imag = [None, None], [None, None]
            for j in range(CH):
                c = chan_ref[j, k]
                u_cos = u_all[k, j, 0:8].astype(F32)
                u_sin = u_all[k, j, 8:16].astype(F32)
                x_cos = slabs[c, 0:8]
                x_sin = slabs[c, 8:16]
                re = u_cos * x_cos + u_sin * x_sin
                im = u_sin * x_cos - u_cos * x_sin
                p = j % 2
                real[p] = re if real[p] is None else real[p] + re
                imag[p] = im if imag[p] is None else imag[p] + im
            z[pl.ds(k, 8, stride=templates + 1), :] = real[0] + real[1]
            z[pl.ds(k + 8 * (templates + 1), 8, stride=templates + 1), :] = imag[0] + imag[1]
        return carry

    for i in range(parts):
        loads[i].wait()
        lax.fori_loop(i * some // step, (i + 1) * some // step, several, 0)

    first = lax.broadcasted_iota(jnp.int32, (templates, LANE), 1) == 0
    base = jnp.float32(CH * NS)
    for column in range(2 * TILES):
        row = column if column < TILES else column - TILES + 8
        weight = jnp.float32(2.0) / base
        if column % TILES == 0:
            weight = jnp.where(first, jnp.float32(1.0), jnp.float32(2.0)) / base
        value = z[row * (templates + 1) : row * (templates + 1) + templates, :] * weight
        packed[:, column * LANE : (column + 1) * LANE] = value.astype(BF16)
    table_copy.wait()
    out_ref[...] = jnp.dot(packed[...], inverse[...], preferred_element_type=F32)


def full(space=pltpu.VMEM):
    return pl.BlockSpec(memory_space=space)


def in_hbm(array):
    return pltpu.with_memory_space_constraint(array, pltpu.HBM)


def on_device(raw, ids, fir, taps, channels, shifts):
    win_count = lax.axis_size("win")
    tmpl_count = lax.axis_size("tmpl")
    win = lax.axis_index("win")
    tmpl = lax.axis_index("tmpl")
    slots, raw_t = raw.shape
    templates = taps.shape[0]
    live = 3 * slots * win_count // 5
    rows = -(-live // 16) * 16
    chan_total = live * tmpl_count
    table = forward_tables()
    inverse = jnp.asarray(inverse_table())
    phase = jnp.asarray(phase_table())

    place = jnp.stack([win, tmpl]).astype(jnp.int32)
    blocks = raw_t // (DEC * BLOCK)
    extra = (NS - WIN_DEV) // BLOCK
    mine = pl.pallas_call(
        spectra_kernel,
        out_shape=[jax.ShapeDtypeStruct((slots, NS), BF16)] * win_count,
        in_specs=[full(pltpu.SMEM)] + [full(pltpu.HBM)] * 3,
        out_specs=[full()] * win_count,
        scratch_shapes=[
            pltpu.VMEM((slots, raw_t + SPAN - DEC * BLOCK), BF16),
            pltpu.VMEM((1, NTAP), BF16),
            pltpu.VMEM((2, NS // 2, NF), BF16),
            pltpu.VMEM(((blocks + extra) * slots, BLOCK), BF16),
            pltpu.VMEM((2, win_count * slots, NS // 2), BF16),
            pltpu.SemaphoreType.DMA((4,)),
        ],
        compiler_params=pltpu.CompilerParams(vmem_limit_bytes=24 * MIB),
        name="spectra",
    )(place, in_hbm(raw), in_hbm(fir[None, :]), in_hbm(jnp.asarray(table)))

    parts = [mine[0]]
    for d in range(1, win_count):
        parts.append(lax.ppermute(mine[d], "win", [(i, i ^ d) for i in range(win_count)]))

    packed_rows = pl.pallas_call(
        functools.partial(compact_kernel, tmpl_count),
        out_shape=jax.ShapeDtypeStruct((rows, NS), BF16),
        in_specs=[full(pltpu.SMEM)] + [full()] * (1 + win_count),
        out_specs=full(),
        scratch_shapes=[pltpu.VMEM((win_count * slots, NS), BF16)],
        compiler_params=pltpu.CompilerParams(vmem_limit_bytes=24 * MIB),
        name="compact",
    )(place, ids[None, :], *parts)

    pair = 6
    slabs, labels = pl.pallas_call(
        functools.partial(template_kernel, slots),
        grid=(CH // pair,),
        out_shape=[
            pltpu.HBM((templates, CH, 16, LANE), BF16),
            pltpu.HBM((tmpl_count, -(-live // LANE) * LANE), jnp.int32),
        ],
        in_specs=[
            full(pltpu.SMEM),
            full(pltpu.HBM),
            full(),
            full(),
            full(),
            full(),
        ],
        out_specs=[
            pl.BlockSpec((templates, pair, 16, LANE), lambda i: (0, i, 0, 0)),
            full(),
        ],
        scratch_shapes=[pltpu.VMEM((pair // 2 * templates * PITCH + 8, LANE), F32)] * 2
        + [pltpu.VMEM((TL, LANE), F32)],
        compiler_params=pltpu.CompilerParams(vmem_limit_bytes=40 * MIB),
        name="templates",
    )(
        shifts.T,
        in_hbm(packed_rows),
        ids[None, :],
        in_hbm(taps.transpose(1, 2, 0)),
        in_hbm(jnp.asarray(table[:, : TL // 2])),
        in_hbm(phase),
    )

    held = {0: packed_rows}
    bit = tmpl_count // 2
    while bit:
        for d in list(held):
            source = held[d]
            if d and bit == 1:
                source, slabs = lax.optimization_barrier((source, slabs))
            held[d | bit] = lax.ppermute(source, "tmpl", [(i, i ^ bit) for i in range(tmpl_count)])
        bit //= 2
    pieces = [held[d] for d in range(tmpl_count)]

    return pl.pallas_call(
        functools.partial(stack_kernel, live),
        out_shape=jax.ShapeDtypeStruct((templates, WIN_DEV), F32),
        in_specs=[full(pltpu.SMEM)] * 3 + [full(pltpu.HBM)] * 2 + [full()] * tmpl_count,
        out_specs=full(),
        scratch_shapes=[
            pltpu.VMEM((templates, CH, 16, LANE), BF16),
            pltpu.VMEM((2 * NF, WIN_DEV), BF16),
            pltpu.VMEM((rows * PITCH + 8, LANE), F32),
            pltpu.VMEM((chan_total, 16, LANE), F32),
            pltpu.VMEM((16 * (templates + 1), LANE), F32),
            pltpu.VMEM((templates, NS), BF16),
            pltpu.SemaphoreType.DMA((9,)),
        ],
        compiler_params=pltpu.CompilerParams(vmem_limit_bytes=(32 if chan_total <= 1024 else 58) * MIB),
        name="stacks",
    )(place, channels.T, labels, in_hbm(slabs), in_hbm(inverse), *pieces)


def solution(mesh):
    return jax.shard_map(
        on_device,
        mesh=mesh,
        in_specs=(
            P(("win", "tmpl"), None),
            P(),
            P(),
            P("tmpl", None, None),
            P("tmpl", None),
            P("tmpl", None),
        ),
        out_specs=P("tmpl", "win"),
        check_vma=False,
    )
```

```python
import functools
import math

import jax
import jax.numpy as jnp
import ml_dtypes
import numpy as np
from jax import lax
from jax.experimental import pallas as pl
from jax.experimental.pallas import tpu as pltpu
from jax.sharding import PartitionSpec as P

WIN_DEV = 1024
TL = 400
CH = 30
DEC = 2
NTAP = 64
MOVE = 256
NS = 1792
NF = 896
LANE = 128
TILES = NF // LANE
BLOCK = 256
SPAN = 640
PITCH = 2 * TILES
GROUP = 3
MIB = 2**20
BF16 = jnp.bfloat16
F32 = jnp.float32


def angles(rows, columns):
    step = np.float32(2.0 * math.pi / NS)
    turns = np.arange(rows)[:, None] * np.arange(columns)[None, :] % NS
    return (turns.astype(np.float32) * step).astype(np.float64)


def order():
    low = np.arange(3 * LANE)
    high = NF - low
    high[0] = NF // 2
    rest = np.arange(3 * LANE, NF // 2)
    return np.concatenate([low, high, rest, NF - rest])


def forward_tables():
    angle = angles(NS, NF)
    cosine, sine = np.cos(angle), np.sin(angle)
    half = NF // 2
    columns = []
    for begin in range(0, half, LANE):
        end = min(begin + LANE, half)
        columns += [cosine[:, begin:end], sine[:, begin:end]]
    table = np.concatenate(columns, axis=1)
    even, odd = table[0::2].copy(), table[1::2].copy()
    even[:, LANE] = cosine[0::2, half]
    odd[:, LANE] = sine[1::2, half]
    return np.stack([even, odd]).astype(ml_dtypes.bfloat16)


def inverse_table():
    angle = angles(NF, WIN_DEV)[order()]
    return np.concatenate([np.cos(angle), -np.sin(angle)], axis=0).astype(ml_dtypes.bfloat16)


def phase_table(versions, coarse):
    angle = angles(versions * coarse, NF)[::coarse, order()]
    slab = np.zeros((versions, 16, LANE), np.float32)
    slab[:, :TILES] = np.cos(angle).reshape(versions, TILES, LANE)
    slab[:, 8 : 8 + TILES] = np.sin(angle).reshape(versions, TILES, LANE)
    return slab


def tile_of(array, column):
    return array[:, column * LANE : (column + 1) * LANE]


def butterfly(q, even, odd):
    lane = lax.broadcasted_iota(jnp.int32, (even.shape[0], LANE), 1)
    if q == 3:
        low, gap = even + odd, even - odd
        left = lane < LANE // 2
        yield 6, jnp.where(left, low, pltpu.roll(gap, LANE // 2, 1))
        yield 13, jnp.where(left, pltpu.roll(low, LANE // 2, 1), -gap)
        return
    low_cos, low_sin = tile_of(even, 0) + tile_of(odd, 0), tile_of(even, 1) + tile_of(odd, 1)
    high_cos, high_sin = tile_of(even, 0) - tile_of(odd, 0), tile_of(odd, 1) - tile_of(even, 1)
    if q == 0:
        low_sin = jnp.where(lane == 0, 0.0, low_sin)
        high_cos = jnp.where(lane == 0, tile_of(even, 1), high_cos)
        high_sin = jnp.where(lane == 0, tile_of(odd, 1), high_sin)
    yield q, low_cos
    yield 7 + q, low_sin
    yield 3 + q, high_cos
    yield 10 + q, high_sin


def columns_of(q):
    return slice(2 * q * LANE, min(2 * (q + 1) * LANE, NF))


def spectra_kernel(place_ref, raw_hbm, fir_hbm, table_hbm, *rest):
    win_count = len(rest) - 6
    outs = rest[:win_count]
    raw, fir, table, filt, tile, sems = rest[win_count:]
    slots, raw_t = raw_hbm.shape
    length = DEC * BLOCK
    blocks = raw_t // length
    raw_copy = pltpu.make_async_copy(raw_hbm, raw.at[:, 0:raw_t], sems.at[0])
    raw_copy.start()
    fir_copy = pltpu.make_async_copy(fir_hbm, fir, sems.at[1])
    fir_copy.start()
    loads = [pltpu.make_async_copy(table_hbm.at[p], table.at[p], sems.at[2 + p]) for p in range(2)]
    for load in loads:
        load.start()
    raw[:, raw_t:] = jnp.zeros((slots, SPAN - length), BF16)
    fir_copy.wait()
    taps = jnp.concatenate([fir[...].astype(F32), jnp.zeros((1, SPAN - NTAP), F32)], axis=1)
    spread = jnp.broadcast_to(taps, (BLOCK // 2, SPAN))
    even = pltpu.roll(spread, 0, 1, stride=2 * DEC, stride_axis=0)
    odd = pltpu.roll(spread, DEC, 1, stride=2 * DEC, stride_axis=0)
    band = jnp.concatenate([even, odd], axis=0).astype(BF16)
    raw_copy.wait()
    segments = jnp.concatenate([raw[:, b * length : b * length + SPAN] for b in range(blocks)], axis=0)
    result = lax.dot_general(segments, band, (((1,), (1,)), ((), ())), preferred_element_type=F32)
    filt[0 : blocks * slots] = result.astype(BF16)
    per_win = WIN_DEV // BLOCK
    per_tile = NS // BLOCK
    filt[blocks * slots :] = jnp.zeros(((per_tile - per_win) * slots, BLOCK), BF16)
    for d in range(win_count):
        first = (place_ref[0] ^ d) * per_win
        for m in range(per_tile):
            start = pl.multiple_of((first + m) * slots, slots)
            block = filt[pl.ds(start, slots), :]
            for p in range(2):
                tile[p, d * slots : (d + 1) * slots, m * LANE : (m + 1) * LANE] = tile_of(block, p)
    values = tile[...].astype(F32)
    scale = lax.rsqrt(jnp.sum(jnp.sum(values * values, axis=2, keepdims=True), axis=0) / NS + 1e-05)
    for load in loads:
        load.wait()
    for q in range(4):
        sums = [jnp.dot(tile[p], table[p, :, columns_of(q)], preferred_element_type=F32) for p in range(2)]
        for column, value in butterfly(q, *sums):
            value = (value * scale).astype(BF16)
            for d in range(win_count):
                outs[d][:, column * LANE : (column + 1) * LANE] = value[d * slots : (d + 1) * slots]


def column_ids(ids, tmpl, tmpl_count, slots):
    total = ids.shape[1]
    count = total // tmpl_count
    source = lax.broadcasted_iota(jnp.int32, (total, count), 0)
    target = lax.broadcasted_iota(jnp.int32, (total, count), 1)
    wanted = (target // slots * tmpl_count + tmpl) * slots + target % slots
    pick = jnp.where(source == wanted, 1.0, 0.0).astype(BF16)
    digits = jnp.concatenate([(ids + 1) // 64, (ids + 1) % 64], axis=0).astype(F32)
    digits = jnp.concatenate([digits, jnp.zeros((14, total), F32)], axis=0).astype(BF16)
    found = jnp.dot(digits, pick, preferred_element_type=F32)
    return found[0:1], found[1:2]


def picks(high, low, rows):
    count = high.shape[1]
    live = high + low > 0.0
    above = lax.broadcasted_iota(jnp.int32, (count, count), 0) < lax.broadcasted_iota(
        jnp.int32, (count, count), 1
    )
    marks = jnp.broadcast_to(jnp.where(live, 1.0, 0.0), (16, count)).astype(BF16)
    rank = jnp.dot(marks, jnp.where(above, 1.0, 0.0).astype(BF16), preferred_element_type=F32)
    rank = jnp.where(live, rank[0:1], -1.0)
    wanted = lax.broadcasted_iota(jnp.int32, (rows, count), 0).astype(F32)
    return jnp.where(wanted == rank, 1.0, 0.0).astype(BF16)


def compact_kernel(tmpl_count, place_ref, ids_ref, *rest):
    blocks, out_ref, data = rest[:-2], rest[-2], rest[-1]
    slots = blocks[0].shape[0]
    high, low = column_ids(ids_ref[...], place_ref[1], tmpl_count, slots)
    pick = picks(high, low, out_ref.shape[0])
    for d, block in enumerate(blocks):
        start = pl.multiple_of((place_ref[0] ^ d) * slots, slots)
        data[pl.ds(start, slots), :] = block[...]
    out_ref[...] = jnp.dot(pick, data[...], preferred_element_type=F32).astype(BF16)


def delayed(wave, shift, most):
    row = lax.broadcasted_iota(jnp.int32, (8, LANE), 0)
    fine = jnp.broadcast_to(shift & 7, (8, LANE))
    keep = row >= fine
    source = (row - fine) & 7
    zero = jnp.zeros((8, LANE), F32)
    turned = [jnp.take_along_axis(wave[i : i + 8], source, axis=0) for i in range(0, wave.shape[0], 8)]
    tiles = [jnp.where(keep, here, above) for here, above in zip(turned + [zero], [zero] + turned)]
    size = 1
    while len(tiles) < most:
        move = jnp.broadcast_to((shift & (8 * size)) != 0, (8, LANE))
        still = tiles + [zero] * size
        moved = [zero] * size + tiles
        tiles = [jnp.where(move, moved[i], still[i]) for i in range(min(len(still), most))]
        size *= 2
    return jnp.concatenate(tiles + [zero] * (-most % 2), axis=0)


def template_kernel(begin, coarse, shift_ref, after_ref, taps_ref, table_ref, u_ref, wave):
    templates = taps_ref.shape[2]
    count = u_ref.shape[0] // (templates * PITCH)
    most = (TL + coarse) // 16

    def load(index):
        halves = [[], []]
        for j in range(index * GROUP, (index + 1) * GROUP):
            wave[...] = taps_ref[j].astype(F32)
            even, odd = wave[pl.ds(0, TL // 2, stride=2), :], wave[pl.ds(1, TL // 2, stride=2), :]
            shift = shift_ref[begin + j : begin + j + 1, :] % coarse
            swap = jnp.broadcast_to((shift & 1) != 0, even.shape)
            halves[0].append(delayed(jnp.where(swap, odd, even), (shift + 1) >> 1, most))
            halves[1].append(delayed(jnp.where(swap, even, odd), shift >> 1, most))
        return [jnp.concatenate([jnp.transpose(h.astype(BF16)) for h in half], axis=0) for half in halves]

    for index in range(count // GROUP):
        halves = load(index)
        for q in range(4):
            sums = [jnp.dot(halves[p], table_ref[p, :, columns_of(q)], preferred_element_type=F32) for p in range(2)]
            for column, value in butterfly(q, *sums):
                for j in range(GROUP):
                    for g in range(templates // 8):
                        at = (g * 8 * count + index * GROUP + j) * PITCH + column
                        part = value[j * templates + g * 8 : j * templates + (g + 1) * 8]
                        u_ref[pl.ds(at, 8, stride=count * PITCH), :] = part


def index_kernel(slots, versions, coarse, ids_ref, channel_ref, shift_ref, label_ref, slab_ref):
    tmpl_count, width = label_ref.shape
    for t in range(tmpl_count):
        high, low = column_ids(ids_ref[...], t, tmpl_count, slots)
        digits = jnp.concatenate([high, low, jnp.zeros((14, high.shape[1]), F32)], axis=0).astype(BF16)
        pick = picks(high, low, width)
        row = lax.dot_general(digits, pick, (((1,), (1,)), ((), ())), preferred_element_type=F32)
        label_ref[t : t + 1, :] = (row[0:1] * 64.0 + row[1:2]).astype(jnp.int32) - 1
    slab_ref[0:CH, :] = channel_ref[...] * versions + shift_ref[...] // coarse
    slab_ref[CH:, :] = jnp.zeros((slab_ref.shape[0] - CH, slab_ref.shape[1]), jnp.int32)


def stack_kernel(live, versions, counts, in_main, place_ref, slab_ref, label_ref, inverse_hbm, phase_ref, *rest):
    u_refs, pieces = rest[: len(counts)], rest[len(counts) : -8]
    out_ref, inverse, flat, slabs, z, packed, held, sems = rest[-8:]
    templates = out_ref.shape[0]
    table_copy = pltpu.make_async_copy(inverse_hbm, inverse, sems.at[0])
    table_copy.start()
    rows = held.shape[0]
    tmpl = place_ref[1]
    flat[rows * PITCH :, :] = jnp.zeros((8, LANE), F32)
    turns = [(phase_ref[a, 0:8], phase_ref[a, 8:16]) for a in range(1, versions)]
    fetches = [pltpu.make_async_copy(pieces[d], held, sems.at[1]) for d in in_main]
    fetches[0].start()
    for d in [d for d in range(len(pieces)) if d not in in_main] + list(in_main):
        piece = pieces[d]
        if d in in_main:
            which = in_main.index(d)
            if which:
                fetches[which].start()
            fetches[which].wait()
            piece = held
        for g in range(rows // 16):
            for column in range(2 * TILES):
                value = piece[g * 16 : (g + 1) * 16, column * LANE : (column + 1) * LANE].astype(F32)
                for h in range(2):
                    flat[pl.ds((2 * g + h) * 8 * PITCH + column, 8, stride=PITCH), :] = value[h * 8 : (h + 1) * 8]
        for r in range(live):
            label = label_ref[tmpl ^ d, r] * versions
            x_cos = flat[r * PITCH : r * PITCH + 8]
            x_sin = flat[r * PITCH + TILES : r * PITCH + TILES + 8]
            slabs[label, 0:8] = x_cos
            slabs[label, 8:16] = x_sin
            for a, (cosine, sine) in enumerate(turns):
                slabs[label + a + 1, 0:8] = x_cos * cosine + x_sin * sine
                slabs[label + a + 1, 8:16] = x_sin * cosine - x_cos * sine

    step = 4

    def several(i, carry):
        for q in range(step):
            k = i * step + q
            real, imag = [None, None], [None, None]
            j = 0
            for u_ref, count in zip(u_refs, counts):
                for own in range(count):
                    c = slab_ref[i * step + (j * templates + q)]
                    at = i * (step * count * PITCH) + (q * count + own) * PITCH
                    u_cos = u_ref[pl.ds(at, 8), :]
                    u_sin = u_ref[pl.ds(at + TILES, 8), :]
                    x_cos = slabs[c, 0:8]
                    x_sin = slabs[c, 8:16]
                    re = u_cos * x_cos + u_sin * x_sin
                    im = u_sin * x_cos - u_cos * x_sin
                    p = j % 2
                    real[p] = re if real[p] is None else real[p] + re
                    imag[p] = im if imag[p] is None else imag[p] + im
                    j += 1
            z[pl.ds(k, 8, stride=templates + 1), :] = real[0] + real[1]
            z[pl.ds(k + 8 * (templates + 1), 8, stride=templates + 1), :] = imag[0] + imag[1]
        return carry

    lax.fori_loop(0, templates // step, several, 0)

    first = lax.broadcasted_iota(jnp.int32, (templates, LANE), 1) == 0
    base = jnp.float32(CH * NS)
    for column in range(2 * TILES):
        row = column if column < TILES else column - TILES + 8
        weight = jnp.float32(2.0) / base
        if column % TILES == 0:
            weight = jnp.where(first, jnp.float32(1.0), jnp.float32(2.0)) / base
        value = z[row * (templates + 1) : row * (templates + 1) + templates, :] * weight
        packed[:, column * LANE : (column + 1) * LANE] = value.astype(BF16)
    table_copy.wait()
    out_ref[...] = jnp.dot(packed[...], inverse[...], preferred_element_type=F32)


def full(space=pltpu.VMEM):
    return pl.BlockSpec(memory_space=space)


def in_hbm(array):
    return pltpu.with_memory_space_constraint(array, pltpu.HBM)


def on_device(raw, ids, fir, taps, channels, shifts):
    win_count = lax.axis_size("win")
    tmpl_count = lax.axis_size("tmpl")
    win = lax.axis_index("win")
    tmpl = lax.axis_index("tmpl")
    slots, raw_t = raw.shape
    templates = taps.shape[0]
    live = 3 * slots * win_count // 5
    rows = -(-live // 16) * 16
    chan_total = live * tmpl_count
    table = forward_tables()
    inverse = jnp.asarray(inverse_table())

    place = jnp.stack([win, tmpl]).astype(jnp.int32)
    blocks = raw_t // (DEC * BLOCK)
    extra = (NS - WIN_DEV) // BLOCK
    mine = pl.pallas_call(
        spectra_kernel,
        out_shape=[jax.ShapeDtypeStruct((slots, NS), BF16)] * win_count,
        in_specs=[full(pltpu.SMEM)] + [full(pltpu.HBM)] * 3,
        out_specs=[full()] * win_count,
        scratch_shapes=[
            pltpu.VMEM((slots, raw_t + SPAN - DEC * BLOCK), BF16),
            pltpu.VMEM((1, NTAP), BF16),
            pltpu.VMEM((2, NS // 2, NF), BF16),
            pltpu.VMEM(((blocks + extra) * slots, BLOCK), BF16),
            pltpu.VMEM((2, win_count * slots, NS // 2), BF16),
            pltpu.SemaphoreType.DMA((4,)),
        ],
        compiler_params=pltpu.CompilerParams(vmem_limit_bytes=24 * MIB),
        name="spectra",
    )(place, in_hbm(raw), in_hbm(fir[None, :]), in_hbm(jnp.asarray(table)))

    parts = [mine[0]]
    for d in range(1, win_count):
        parts.append(lax.ppermute(mine[d], "win", [(i, i ^ d) for i in range(win_count)]))

    packed_rows = pl.pallas_call(
        functools.partial(compact_kernel, tmpl_count),
        out_shape=jax.ShapeDtypeStruct((rows, NS), BF16),
        in_specs=[full(pltpu.SMEM)] + [full()] * (1 + win_count),
        out_specs=full(),
        scratch_shapes=[pltpu.VMEM((win_count * slots, NS), BF16)],
        compiler_params=pltpu.CompilerParams(vmem_limit_bytes=24 * MIB),
        name="compact",
    )(place, ids[None, :], *parts)

    small = chan_total <= 1024
    versions, coarse = (3, 112) if small else (1, MOVE)
    labels, slab_index = pl.pallas_call(
        functools.partial(index_kernel, slots, versions, coarse),
        out_shape=[
            pltpu.HBM((tmpl_count, -(-live // LANE) * LANE), jnp.int32),
            pltpu.HBM((32, templates), jnp.int32),
        ],
        in_specs=[full()] * 3,
        out_specs=[full()] * 2,
        compiler_params=pltpu.CompilerParams(vmem_limit_bytes=8 * MIB),
        name="indices",
    )(ids[None, :], channels.T, shifts.T)

    waves = taps.transpose(1, 2, 0)
    reach = -(-(TL + coarse) // 32) * 16
    counts = (18, 12)
    spectra_of = []
    for n, count in enumerate(counts):
        begin = sum(counts[:n])
        spectra_of.append(
            pl.pallas_call(
                functools.partial(template_kernel, begin, coarse),
                out_shape=jax.ShapeDtypeStruct((templates * count * PITCH + 8, LANE), F32),
                grid=(1,),
                in_specs=[
                    full(),
                    full(pltpu.HBM),
                    pl.BlockSpec((pl.Element(count), pl.Element(TL), pl.Element(templates)), lambda i, begin=begin: (begin, 0, 0)),
                    full(),
                ],
                out_specs=full(),
                scratch_shapes=[pltpu.VMEM((TL, LANE), F32)],
                compiler_params=pltpu.CompilerParams(vmem_limit_bytes=(12 if small else 40) * MIB),
                name="templates",
            )(shifts.T, in_hbm(packed_rows), in_hbm(waves), in_hbm(jnp.asarray(table[:, :reach])))
        )

    held = {0: packed_rows}
    bit = tmpl_count // 2
    while bit:
        for d in list(held):
            source = held[d]
            if d and bit == 1:
                source, spectra_of[0] = lax.optimization_barrier((source, spectra_of[0]))
            held[d | bit] = lax.ppermute(source, "tmpl", [(i, i ^ bit) for i in range(tmpl_count)])
        bit //= 2
    pieces = [held[d] for d in range(tmpl_count)]

    in_main = (0,) if small else tuple(range(tmpl_count))
    places = [pltpu.HBM if d in in_main else pltpu.VMEM for d in range(tmpl_count)]
    return pl.pallas_call(
        functools.partial(stack_kernel, live, versions, counts, in_main),
        out_shape=jax.ShapeDtypeStruct((templates, WIN_DEV), F32),
        in_specs=[full(pltpu.SMEM)] * 3
        + [full(pltpu.HBM), full()]
        + [full()] * len(counts)
        + [full(space) for space in places],
        out_specs=full(),
        scratch_shapes=[
            pltpu.VMEM((2 * NF, WIN_DEV), BF16),
            pltpu.VMEM((rows * PITCH + 8, LANE), F32),
            pltpu.VMEM((chan_total * versions, 16, LANE), F32),
            pltpu.VMEM((16 * (templates + 1), LANE), F32),
            pltpu.VMEM((templates, NS), BF16),
            pltpu.VMEM((rows, NS), BF16),
            pltpu.SemaphoreType.DMA((2,)),
        ],
        compiler_params=pltpu.CompilerParams(vmem_limit_bytes=(19 if small else 58) * MIB),
        name="stacks",
    )(
        place,
        in_hbm(slab_index.reshape(-1)),
        in_hbm(labels),
        in_hbm(inverse),
        jnp.asarray(phase_table(versions, coarse)),
        *spectra_of,
        *[in_hbm(piece) if d in in_main else piece for d, piece in enumerate(pieces)],
    )


def solution(mesh):
    return jax.shard_map(
        on_device,
        mesh=mesh,
        in_specs=(
            P(("win", "tmpl"), None),
            P(),
            P(),
            P("tmpl", None, None),
            P("tmpl", None),
            P("tmpl", None),
        ),
        out_specs=P("tmpl", "win"),
        check_vma=False,
    )
```

```python
import functools
import math

import jax
import jax.numpy as jnp
import ml_dtypes
import numpy as np
from jax import lax
from jax.experimental import pallas as pl
from jax.experimental.pallas import tpu as pltpu
from jax.sharding import PartitionSpec as P

WIN_DEV = 1024
TL = 400
CH = 30
DEC = 2
NTAP = 64
MOVE = 256
NS = 1792
NF = 896
LANE = 128
TILES = NF // LANE
BLOCK = 256
SPAN = 640
PITCH = 2 * TILES
GROUP = 3
MIB = 2**20
BF16 = jnp.bfloat16
F32 = jnp.float32


def angles(rows, columns):
    step = np.float32(2.0 * math.pi / NS)
    turns = np.arange(rows)[:, None] * np.arange(columns)[None, :] % NS
    return (turns.astype(np.float32) * step).astype(np.float64)


def order():
    low = np.arange(3 * LANE)
    high = NF - low
    high[0] = NF // 2
    rest = np.arange(3 * LANE, NF // 2)
    return np.concatenate([low, high, rest, NF - rest])


def forward_tables():
    angle = angles(NS, NF)
    cosine, sine = np.cos(angle), np.sin(angle)
    half = NF // 2
    columns = []
    for begin in range(0, half, LANE):
        end = min(begin + LANE, half)
        columns += [cosine[:, begin:end], sine[:, begin:end]]
    table = np.concatenate(columns, axis=1)
    even, odd = table[0::2].copy(), table[1::2].copy()
    even[:, LANE] = cosine[0::2, half]
    odd[:, LANE] = sine[1::2, half]
    return np.stack([even, odd]).astype(ml_dtypes.bfloat16)


def inverse_table():
    angle = angles(NF, WIN_DEV)[order()]
    return np.concatenate([np.cos(angle), -np.sin(angle)], axis=0).astype(ml_dtypes.bfloat16)


def phase_table(versions, coarse):
    angle = angles(versions * coarse, NF)[::coarse, order()]
    slab = np.zeros((versions, 16, LANE), np.float32)
    slab[:, :TILES] = np.cos(angle).reshape(versions, TILES, LANE)
    slab[:, 8 : 8 + TILES] = np.sin(angle).reshape(versions, TILES, LANE)
    return slab


def tile_of(array, column):
    return array[:, column * LANE : (column + 1) * LANE]


def butterfly(q, even, odd):
    lane = lax.broadcasted_iota(jnp.int32, (even.shape[0], LANE), 1)
    if q == 3:
        low, gap = even + odd, even - odd
        left = lane < LANE // 2
        yield 6, jnp.where(left, low, pltpu.roll(gap, LANE // 2, 1))
        yield 13, jnp.where(left, pltpu.roll(low, LANE // 2, 1), -gap)
        return
    low_cos, low_sin = tile_of(even, 0) + tile_of(odd, 0), tile_of(even, 1) + tile_of(odd, 1)
    high_cos, high_sin = tile_of(even, 0) - tile_of(odd, 0), tile_of(odd, 1) - tile_of(even, 1)
    if q == 0:
        low_sin = jnp.where(lane == 0, 0.0, low_sin)
        high_cos = jnp.where(lane == 0, tile_of(even, 1), high_cos)
        high_sin = jnp.where(lane == 0, tile_of(odd, 1), high_sin)
    yield q, low_cos
    yield 7 + q, low_sin
    yield 3 + q, high_cos
    yield 10 + q, high_sin


def columns_of(q):
    return slice(2 * q * LANE, min(2 * (q + 1) * LANE, NF))


def spectra_kernel(raw_hbm, fir_hbm, table_hbm, *rest):
    win_count = len(rest) - 6
    outs = rest[:win_count]
    raw, fir, table, filt, tile, sems = rest[win_count:]
    win = lax.axis_index("win")
    slots, raw_t = raw_hbm.shape
    length = DEC * BLOCK
    blocks = raw_t // length
    raw_copy = pltpu.make_async_copy(raw_hbm, raw.at[:, 0:raw_t], sems.at[0])
    raw_copy.start()
    fir_copy = pltpu.make_async_copy(fir_hbm, fir, sems.at[1])
    fir_copy.start()
    loads = [pltpu.make_async_copy(table_hbm.at[p], table.at[p], sems.at[2 + p]) for p in range(2)]
    for load in loads:
        load.start()
    raw[:, raw_t:] = jnp.zeros((slots, SPAN - length), BF16)
    fir_copy.wait()
    taps = jnp.concatenate([fir[...].astype(F32), jnp.zeros((1, SPAN - NTAP), F32)], axis=1)
    spread = jnp.broadcast_to(taps, (BLOCK // 2, SPAN))
    even = pltpu.roll(spread, 0, 1, stride=2 * DEC, stride_axis=0)
    odd = pltpu.roll(spread, DEC, 1, stride=2 * DEC, stride_axis=0)
    band = jnp.concatenate([even, odd], axis=0).astype(BF16)
    raw_copy.wait()
    segments = jnp.concatenate([raw[:, b * length : b * length + SPAN] for b in range(blocks)], axis=0)
    result = lax.dot_general(segments, band, (((1,), (1,)), ((), ())), preferred_element_type=F32)
    filt[0 : blocks * slots] = result.astype(BF16)
    per_win = WIN_DEV // BLOCK
    per_tile = NS // BLOCK
    filt[blocks * slots :] = jnp.zeros(((per_tile - per_win) * slots, BLOCK), BF16)
    for d in range(win_count):
        first = (win ^ d) * per_win
        for m in range(per_tile):
            start = pl.multiple_of((first + m) * slots, slots)
            block = filt[pl.ds(start, slots), :]
            for p in range(2):
                tile[p, d * slots : (d + 1) * slots, m * LANE : (m + 1) * LANE] = tile_of(block, p)
    values = tile[...].astype(F32)
    scale = lax.rsqrt(jnp.sum(jnp.sum(values * values, axis=2, keepdims=True), axis=0) / NS + 1e-05)
    for load in loads:
        load.wait()
    for q in range(4):
        sums = [jnp.dot(tile[p], table[p, :, columns_of(q)], preferred_element_type=F32) for p in range(2)]
        for column, value in butterfly(q, *sums):
            value = (value * scale).astype(BF16)
            for d in range(win_count):
                outs[d][:, column * LANE : (column + 1) * LANE] = value[d * slots : (d + 1) * slots]


def column_ids(ids, tmpl, tmpl_count, slots):
    total = ids.shape[1]
    count = total // tmpl_count
    source = lax.broadcasted_iota(jnp.int32, (total, count), 0)
    target = lax.broadcasted_iota(jnp.int32, (total, count), 1)
    wanted = (target // slots * tmpl_count + tmpl) * slots + target % slots
    pick = jnp.where(source == wanted, 1.0, 0.0).astype(BF16)
    digits = jnp.concatenate([(ids + 1) // 64, (ids + 1) % 64], axis=0).astype(F32)
    digits = jnp.concatenate([digits, jnp.zeros((14, total), F32)], axis=0).astype(BF16)
    found = jnp.dot(digits, pick, preferred_element_type=F32)
    return found[0:1], found[1:2]


def picks(high, low, rows):
    count = high.shape[1]
    live = high + low > 0.0
    above = lax.broadcasted_iota(jnp.int32, (count, count), 0) < lax.broadcasted_iota(
        jnp.int32, (count, count), 1
    )
    marks = jnp.broadcast_to(jnp.where(live, 1.0, 0.0), (16, count)).astype(BF16)
    rank = jnp.dot(marks, jnp.where(above, 1.0, 0.0).astype(BF16), preferred_element_type=F32)
    rank = jnp.where(live, rank[0:1], -1.0)
    wanted = lax.broadcasted_iota(jnp.int32, (rows, count), 0).astype(F32)
    return jnp.where(wanted == rank, 1.0, 0.0).astype(BF16)


def compact_kernel(ids_ref, *rest):
    blocks, out_ref, data = rest[:-2], rest[-2], rest[-1]
    slots = blocks[0].shape[0]
    win = lax.axis_index("win")
    high, low = column_ids(ids_ref[...], lax.axis_index("tmpl"), lax.axis_size("tmpl"), slots)
    pick = picks(high, low, out_ref.shape[0])
    for d, block in enumerate(blocks):
        start = pl.multiple_of((win ^ d) * slots, slots)
        data[pl.ds(start, slots), :] = block[...]
    out_ref[...] = jnp.dot(pick, data[...], preferred_element_type=F32).astype(BF16)


def delayed(wave, shift, most):
    row = lax.broadcasted_iota(jnp.int32, (8, LANE), 0)
    fine = jnp.broadcast_to(shift & 7, (8, LANE))
    keep = row >= fine
    source = (row - fine) & 7
    zero = jnp.zeros((8, LANE), F32)
    turned = [jnp.take_along_axis(wave[i : i + 8], source, axis=0) for i in range(0, wave.shape[0], 8)]
    tiles = [jnp.where(keep, here, above) for here, above in zip(turned + [zero], [zero] + turned)]
    size = 1
    while len(tiles) < most:
        move = jnp.broadcast_to((shift & (8 * size)) != 0, (8, LANE))
        still = tiles + [zero] * size
        moved = [zero] * size + tiles
        tiles = [jnp.where(move, moved[i], still[i]) for i in range(min(len(still), most))]
        size *= 2
    return jnp.concatenate(tiles + [zero] * (-most % 2), axis=0)


def template_kernel(begin, coarse, shift_ref, after_ref, taps_hbm, table_hbm, u_ref, taps, table, wave, sems):
    count, _, templates = taps.shape
    most = (TL + coarse) // 16
    loads = []
    for index in range(count // GROUP):
        here = slice(index * GROUP, (index + 1) * GROUP)
        there = slice(begin + index * GROUP, begin + (index + 1) * GROUP)
        loads.append(pltpu.make_async_copy(taps_hbm.at[there], taps.at[here], sems.at[index + 1]))
    table_load = pltpu.make_async_copy(table_hbm, table, sems.at[0])
    loads[0].start()
    table_load.start()
    for load in loads[1:]:
        load.start()

    def halves_of(index):
        halves = [[], []]
        for j in range(index * GROUP, (index + 1) * GROUP):
            wave[...] = taps[j].astype(F32)
            even, odd = wave[pl.ds(0, TL // 2, stride=2), :], wave[pl.ds(1, TL // 2, stride=2), :]
            shift = shift_ref[begin + j : begin + j + 1, :] % coarse
            swap = jnp.broadcast_to((shift & 1) != 0, even.shape)
            halves[0].append(delayed(jnp.where(swap, odd, even), (shift + 1) >> 1, most))
            halves[1].append(delayed(jnp.where(swap, even, odd), shift >> 1, most))
        return [jnp.concatenate([jnp.transpose(h.astype(BF16)) for h in half], axis=0) for half in halves]

    for index in range(count // GROUP):
        loads[index].wait()
        halves = halves_of(index)
        if index == 0:
            table_load.wait()
        for q in range(4):
            sums = [jnp.dot(halves[p], table[p, :, columns_of(q)], preferred_element_type=F32) for p in range(2)]
            for column, value in butterfly(q, *sums):
                for j in range(GROUP):
                    for g in range(templates // 8):
                        at = (g * 8 * count + index * GROUP + j) * PITCH + column
                        part = value[j * templates + g * 8 : j * templates + (g + 1) * 8]
                        u_ref[pl.ds(at, 8, stride=count * PITCH), :] = part


def index_kernel(slots, versions, coarse, ids_ref, channel_ref, shift_ref, label_ref, slab_ref):
    tmpl_count, width = label_ref.shape
    for t in range(tmpl_count):
        high, low = column_ids(ids_ref[...], t, tmpl_count, slots)
        digits = jnp.concatenate([high, low, jnp.zeros((14, high.shape[1]), F32)], axis=0).astype(BF16)
        pick = picks(high, low, width)
        row = lax.dot_general(digits, pick, (((1,), (1,)), ((), ())), preferred_element_type=F32)
        label_ref[t : t + 1, :] = (row[0:1] * 64.0 + row[1:2]).astype(jnp.int32) - 1
    slab_ref[0:CH, :] = channel_ref[...] * versions + shift_ref[...] // coarse
    slab_ref[CH:, :] = jnp.zeros((slab_ref.shape[0] - CH, slab_ref.shape[1]), jnp.int32)


def stack_kernel(live, versions, counts, in_main, slab_ref, label_ref, inverse_hbm, phase_ref, *rest):
    u_refs, pieces = rest[: len(counts)], rest[len(counts) : -8]
    out_ref, inverse, flat, slabs, z, packed, held, sems = rest[-8:]
    templates = out_ref.shape[0]
    table_copy = pltpu.make_async_copy(inverse_hbm, inverse, sems.at[0])
    table_copy.start()
    rows = held.shape[0]
    tmpl = lax.axis_index("tmpl")
    flat[rows * PITCH :, :] = jnp.zeros((8, LANE), F32)
    turns = [(phase_ref[a, 0:8], phase_ref[a, 8:16]) for a in range(1, versions)]
    fetches = [pltpu.make_async_copy(pieces[d], held, sems.at[1]) for d in in_main]
    fetches[0].start()
    for d in [d for d in range(len(pieces)) if d not in in_main] + list(in_main):
        piece = pieces[d]
        if d in in_main:
            which = in_main.index(d)
            if which:
                fetches[which].start()
            fetches[which].wait()
            piece = held
        for g in range(rows // 16):
            for column in range(2 * TILES):
                value = piece[g * 16 : (g + 1) * 16, column * LANE : (column + 1) * LANE].astype(F32)
                for h in range(2):
                    flat[pl.ds((2 * g + h) * 8 * PITCH + column, 8, stride=PITCH), :] = value[h * 8 : (h + 1) * 8]
        for r in range(live):
            label = label_ref[tmpl ^ d, r] * versions
            x_cos = flat[r * PITCH : r * PITCH + 8]
            x_sin = flat[r * PITCH + TILES : r * PITCH + TILES + 8]
            slabs[label, 0:8] = x_cos
            slabs[label, 8:16] = x_sin
            for a, (cosine, sine) in enumerate(turns):
                slabs[label + a + 1, 0:8] = x_cos * cosine + x_sin * sine
                slabs[label + a + 1, 8:16] = x_sin * cosine - x_cos * sine

    step = 4

    def several(i, carry):
        for q in range(step):
            k = i * step + q
            real, imag = [None, None], [None, None]
            j = 0
            for u_ref, count in zip(u_refs, counts):
                for own in range(count):
                    c = slab_ref[i * step + (j * templates + q)]
                    at = i * (step * count * PITCH) + (q * count + own) * PITCH
                    u_cos = u_ref[pl.ds(at, 8), :]
                    u_sin = u_ref[pl.ds(at + TILES, 8), :]
                    x_cos = slabs[c, 0:8]
                    x_sin = slabs[c, 8:16]
                    re = u_cos * x_cos + u_sin * x_sin
                    im = u_sin * x_cos - u_cos * x_sin
                    p = j % 2
                    real[p] = re if real[p] is None else real[p] + re
                    imag[p] = im if imag[p] is None else imag[p] + im
                    j += 1
            z[pl.ds(k, 8, stride=templates + 1), :] = real[0] + real[1]
            z[pl.ds(k + 8 * (templates + 1), 8, stride=templates + 1), :] = imag[0] + imag[1]
        return carry

    lax.fori_loop(0, templates // step, several, 0)

    first = lax.broadcasted_iota(jnp.int32, (templates, LANE), 1) == 0
    base = jnp.float32(CH * NS)
    for column in range(2 * TILES):
        row = column if column < TILES else column - TILES + 8
        weight = jnp.float32(2.0) / base
        if column % TILES == 0:
            weight = jnp.where(first, jnp.float32(1.0), jnp.float32(2.0)) / base
        value = z[row * (templates + 1) : row * (templates + 1) + templates, :] * weight
        packed[:, column * LANE : (column + 1) * LANE] = value.astype(BF16)
    table_copy.wait()
    out_ref[...] = jnp.dot(packed[...], inverse[...], preferred_element_type=F32)


def full(space=pltpu.VMEM):
    return pl.BlockSpec(memory_space=space)


def in_hbm(array):
    return pltpu.with_memory_space_constraint(array, pltpu.HBM)


def on_device(raw, ids, fir, taps, channels, shifts):
    win_count = lax.axis_size("win")
    tmpl_count = lax.axis_size("tmpl")
    slots, raw_t = raw.shape
    templates = taps.shape[0]
    live = 3 * slots * win_count // 5
    rows = -(-live // 16) * 16
    chan_total = live * tmpl_count
    table = forward_tables()
    inverse = jnp.asarray(inverse_table())

    blocks = raw_t // (DEC * BLOCK)
    extra = (NS - WIN_DEV) // BLOCK
    mine = pl.pallas_call(
        spectra_kernel,
        out_shape=[jax.ShapeDtypeStruct((slots, NS), BF16)] * win_count,
        in_specs=[full(pltpu.HBM)] * 3,
        out_specs=[full()] * win_count,
        scratch_shapes=[
            pltpu.VMEM((slots, raw_t + SPAN - DEC * BLOCK), BF16),
            pltpu.VMEM((1, NTAP), BF16),
            pltpu.VMEM((2, NS // 2, NF), BF16),
            pltpu.VMEM(((blocks + extra) * slots, BLOCK), BF16),
            pltpu.VMEM((2, win_count * slots, NS // 2), BF16),
            pltpu.SemaphoreType.DMA((4,)),
        ],
        compiler_params=pltpu.CompilerParams(vmem_limit_bytes=24 * MIB),
        name="spectra",
    )(in_hbm(raw), in_hbm(fir[None, :]), in_hbm(jnp.asarray(table)))

    small = chan_total <= 1024
    versions, coarse = (3, 112) if small else (1, MOVE)
    waves = in_hbm(taps.transpose(1, 2, 0))
    reach = -(-(TL + coarse) // 32) * 16
    head = in_hbm(jnp.asarray(table[:, :reach]))
    counts = (12, 18)

    def template_spectra(n, after):
        count = counts[n]
        return pl.pallas_call(
            functools.partial(template_kernel, sum(counts[:n]), coarse),
            out_shape=jax.ShapeDtypeStruct((templates * count * PITCH + 8, LANE), F32),
            in_specs=[full()] + [full(pl.ANY)] + [full(pltpu.HBM)] * 2,
            out_specs=full(),
            scratch_shapes=[
                pltpu.VMEM((count, TL, templates), BF16),
                pltpu.VMEM((2, reach, NF), BF16),
                pltpu.VMEM((TL, LANE), F32),
                pltpu.SemaphoreType.DMA((1 + count // GROUP,)),
            ],
            compiler_params=pltpu.CompilerParams(vmem_limit_bytes=(12 if small else 40) * MIB),
            name="templates",
        )(shifts.T, after, waves, head)

    def exchanged(block, d):
        return lax.ppermute(block, "win", [(i, i ^ d) for i in range(win_count)])

    parts = {0: mine[0]}
    for d in range(win_count - 1, 2, -1):
        parts[d] = exchanged(mine[d], d)
    early = template_spectra(0, mine[0])
    *near, early = lax.optimization_barrier((mine[2], mine[1], early))
    for d, block in zip((2, 1), near):
        parts[d] = exchanged(block, d)
    parts = [parts[d] for d in range(win_count)]

    packed_rows = pl.pallas_call(
        compact_kernel,
        out_shape=jax.ShapeDtypeStruct((rows, NS), BF16),
        in_specs=[full()] * (1 + win_count),
        out_specs=full(),
        scratch_shapes=[pltpu.VMEM((win_count * slots, NS), BF16)],
        compiler_params=pltpu.CompilerParams(vmem_limit_bytes=24 * MIB),
        name="compact",
    )(ids[None, :], *parts)

    late = template_spectra(1, packed_rows)
    labels, slab_index = pl.pallas_call(
        functools.partial(index_kernel, slots, versions, coarse),
        out_shape=[
            pltpu.HBM((tmpl_count, -(-live // LANE) * LANE), jnp.int32),
            pltpu.HBM((32, templates), jnp.int32),
        ],
        in_specs=[full()] * 3,
        out_specs=[full()] * 2,
        compiler_params=pltpu.CompilerParams(vmem_limit_bytes=8 * MIB),
        name="indices",
    )(ids[None, :], channels.T, shifts.T)

    held = {0: packed_rows}
    bit = tmpl_count // 2
    while bit:
        for d in list(held):
            source = held[d]
            if d and bit == 1:
                source, late = lax.optimization_barrier((source, late))
            held[d | bit] = lax.ppermute(source, "tmpl", [(i, i ^ bit) for i in range(tmpl_count)])
        bit //= 2
    pieces = [held[d] for d in range(tmpl_count)]

    in_main = (0,) if small else tuple(range(tmpl_count))
    places = [pltpu.HBM if d in in_main else pltpu.VMEM for d in range(tmpl_count)]
    return pl.pallas_call(
        functools.partial(stack_kernel, live, versions, counts, in_main),
        out_shape=jax.ShapeDtypeStruct((templates, WIN_DEV), F32),
        in_specs=[full(pltpu.SMEM)] * 2
        + [full(pltpu.HBM), full()]
        + [full()] * len(counts)
        + [full(space) for space in places],
        out_specs=full(),
        scratch_shapes=[
            pltpu.VMEM((2 * NF, WIN_DEV), BF16),
            pltpu.VMEM((rows * PITCH + 8, LANE), F32),
            pltpu.VMEM((chan_total * versions, 16, LANE), F32),
            pltpu.VMEM((16 * (templates + 1), LANE), F32),
            pltpu.VMEM((templates, NS), BF16),
            pltpu.VMEM((rows, NS), BF16),
            pltpu.SemaphoreType.DMA((2,)),
        ],
        compiler_params=pltpu.CompilerParams(vmem_limit_bytes=(19 if small else 58) * MIB),
        name="stacks",
    )(
        in_hbm(slab_index.reshape(-1)),
        in_hbm(labels),
        in_hbm(inverse),
        jnp.asarray(phase_table(versions, coarse)),
        early,
        late,
        *[in_hbm(piece) if d in in_main else piece for d, piece in enumerate(pieces)],
    )


def solution(mesh):
    return jax.shard_map(
        on_device,
        mesh=mesh,
        in_specs=(
            P(("win", "tmpl"), None),
            P(),
            P(),
            P("tmpl", None, None),
            P("tmpl", None),
            P("tmpl", None),
        ),
        out_specs=P("tmpl", "win"),
        check_vma=False,
    )
```

```python
import functools
import math

import jax
import jax.numpy as jnp
import ml_dtypes
import numpy as np
from jax import lax
from jax.experimental import pallas as pl
from jax.experimental.pallas import tpu as pltpu
from jax.sharding import PartitionSpec as P

WIN_DEV = 1024
TL = 400
CH = 30
DEC = 2
NTAP = 64
MOVE = 256
NS = 1792
NF = 896
LANE = 128
TILES = NF // LANE
BLOCK = 256
SPAN = 640
PITCH = 2 * TILES
GROUP = 3
MIB = 2**20
BF16 = jnp.bfloat16
F32 = jnp.float32


def angles(rows, columns):
    step = np.float32(2.0 * math.pi / NS)
    turns = np.arange(rows)[:, None] * np.arange(columns)[None, :] % NS
    return (turns.astype(np.float32) * step).astype(np.float64)


def order():
    low = np.arange(3 * LANE)
    high = NF - low
    high[0] = NF // 2
    rest = np.arange(3 * LANE, NF // 2)
    return np.concatenate([low, high, rest, NF - rest])


def forward_tables():
    angle = angles(NS, NF)
    cosine, sine = np.cos(angle), np.sin(angle)
    half = NF // 2
    columns = []
    for begin in range(0, half, LANE):
        end = min(begin + LANE, half)
        columns += [cosine[:, begin:end], sine[:, begin:end]]
    table = np.concatenate(columns, axis=1)
    even, odd = table[0::2].copy(), table[1::2].copy()
    even[:, LANE] = cosine[0::2, half]
    odd[:, LANE] = sine[1::2, half]
    return np.stack([even, odd]).astype(ml_dtypes.bfloat16)


def inverse_table():
    angle = angles(NF, WIN_DEV)[order()]
    return np.concatenate([np.cos(angle), -np.sin(angle)], axis=0).astype(ml_dtypes.bfloat16)


def phase_table(versions, coarse):
    angle = angles(versions * coarse, NF)[::coarse, order()]
    slab = np.zeros((versions, 16, LANE), np.float32)
    slab[:, :TILES] = np.cos(angle).reshape(versions, TILES, LANE)
    slab[:, 8 : 8 + TILES] = np.sin(angle).reshape(versions, TILES, LANE)
    return slab


def tile_of(array, column):
    return array[:, column * LANE : (column + 1) * LANE]


def butterfly(q, even, odd):
    lane = lax.broadcasted_iota(jnp.int32, (even.shape[0], LANE), 1)
    if q == 3:
        low, gap = even + odd, even - odd
        left = lane < LANE // 2
        yield 6, jnp.where(left, low, pltpu.roll(gap, LANE // 2, 1))
        yield 13, jnp.where(left, pltpu.roll(low, LANE // 2, 1), -gap)
        return
    low_cos, low_sin = tile_of(even, 0) + tile_of(odd, 0), tile_of(even, 1) + tile_of(odd, 1)
    high_cos, high_sin = tile_of(even, 0) - tile_of(odd, 0), tile_of(odd, 1) - tile_of(even, 1)
    if q == 0:
        low_sin = jnp.where(lane == 0, 0.0, low_sin)
        high_cos = jnp.where(lane == 0, tile_of(even, 1), high_cos)
        high_sin = jnp.where(lane == 0, tile_of(odd, 1), high_sin)
    yield q, low_cos
    yield 7 + q, low_sin
    yield 3 + q, high_cos
    yield 10 + q, high_sin


def columns_of(q):
    return slice(2 * q * LANE, min(2 * (q + 1) * LANE, NF))


def spectra_kernel(raw_hbm, fir_hbm, table_hbm, *rest):
    win_count = len(rest) - 6
    outs = rest[:win_count]
    raw, fir, table, filt, tile, sems = rest[win_count:]
    win = lax.axis_index("win")
    slots, raw_t = raw_hbm.shape
    length = DEC * BLOCK
    blocks = raw_t // length
    raw_copy = pltpu.make_async_copy(raw_hbm, raw.at[:, 0:raw_t], sems.at[0])
    raw_copy.start()
    fir_copy = pltpu.make_async_copy(fir_hbm, fir, sems.at[1])
    fir_copy.start()
    loads = [pltpu.make_async_copy(table_hbm.at[p], table.at[p], sems.at[2 + p]) for p in range(2)]
    for load in loads:
        load.start()
    raw[:, raw_t:] = jnp.zeros((slots, SPAN - length), BF16)
    fir_copy.wait()
    taps = jnp.concatenate([fir[...].astype(F32), jnp.zeros((1, SPAN - NTAP), F32)], axis=1)
    spread = jnp.broadcast_to(taps, (BLOCK // 2, SPAN))
    even = pltpu.roll(spread, 0, 1, stride=2 * DEC, stride_axis=0)
    odd = pltpu.roll(spread, DEC, 1, stride=2 * DEC, stride_axis=0)
    band = jnp.concatenate([even, odd], axis=0).astype(BF16)
    raw_copy.wait()
    segments = jnp.concatenate([raw[:, b * length : b * length + SPAN] for b in range(blocks)], axis=0)
    result = lax.dot_general(segments, band, (((1,), (1,)), ((), ())), preferred_element_type=F32)
    filt[0 : blocks * slots] = result.astype(BF16)
    per_win = WIN_DEV // BLOCK
    per_tile = NS // BLOCK
    filt[blocks * slots :] = jnp.zeros(((per_tile - per_win) * slots, BLOCK), BF16)
    for d in range(win_count):
        first = (win ^ d) * per_win
        for m in range(per_tile):
            start = pl.multiple_of((first + m) * slots, slots)
            block = filt[pl.ds(start, slots), :]
            for p in range(2):
                tile[p, d * slots : (d + 1) * slots, m * LANE : (m + 1) * LANE] = tile_of(block, p)
    values = tile[...].astype(F32)
    scale = lax.rsqrt(jnp.sum(jnp.sum(values * values, axis=2, keepdims=True), axis=0) / NS + 1e-05)
    for load in loads:
        load.wait()
    for q in range(4):
        sums = [jnp.dot(tile[p], table[p, :, columns_of(q)], preferred_element_type=F32) for p in range(2)]
        for column, value in butterfly(q, *sums):
            value = (value * scale).astype(BF16)
            for d in range(win_count):
                outs[d][:, column * LANE : (column + 1) * LANE] = value[d * slots : (d + 1) * slots]


def column_ids(ids, tmpl, tmpl_count, slots):
    total = ids.shape[1]
    count = total // tmpl_count
    source = lax.broadcasted_iota(jnp.int32, (total, count), 0)
    target = lax.broadcasted_iota(jnp.int32, (total, count), 1)
    wanted = (target // slots * tmpl_count + tmpl) * slots + target % slots
    pick = jnp.where(source == wanted, 1.0, 0.0).astype(BF16)
    digits = jnp.concatenate([(ids + 1) // 64, (ids + 1) % 64], axis=0).astype(F32)
    digits = jnp.concatenate([digits, jnp.zeros((14, total), F32)], axis=0).astype(BF16)
    found = jnp.dot(digits, pick, preferred_element_type=F32)
    return found[0:1], found[1:2]


def picks(high, low, rows):
    count = high.shape[1]
    live = high + low > 0.0
    above = lax.broadcasted_iota(jnp.int32, (count, count), 0) < lax.broadcasted_iota(
        jnp.int32, (count, count), 1
    )
    marks = jnp.broadcast_to(jnp.where(live, 1.0, 0.0), (16, count)).astype(BF16)
    rank = jnp.dot(marks, jnp.where(above, 1.0, 0.0).astype(BF16), preferred_element_type=F32)
    rank = jnp.where(live, rank[0:1], -1.0)
    wanted = lax.broadcasted_iota(jnp.int32, (rows, count), 0).astype(F32)
    return jnp.where(wanted == rank, 1.0, 0.0).astype(BF16)


def compact_kernel(ids_ref, *rest):
    blocks, out_ref, data = rest[:-2], rest[-2], rest[-1]
    slots = blocks[0].shape[0]
    win = lax.axis_index("win")
    high, low = column_ids(ids_ref[...], lax.axis_index("tmpl"), lax.axis_size("tmpl"), slots)
    pick = picks(high, low, out_ref.shape[0])
    for d, block in enumerate(blocks):
        start = pl.multiple_of((win ^ d) * slots, slots)
        data[pl.ds(start, slots), :] = block[...]
    out_ref[...] = jnp.dot(pick, data[...], preferred_element_type=F32).astype(BF16)


def delayed(wave, shift, most):
    row = lax.broadcasted_iota(jnp.int32, (8, LANE), 0)
    fine = jnp.broadcast_to(shift & 7, (8, LANE))
    keep = row >= fine
    source = (row - fine) & 7
    zero = jnp.zeros((8, LANE), F32)
    turned = [jnp.take_along_axis(wave[i : i + 8], source, axis=0) for i in range(0, wave.shape[0], 8)]
    tiles = [jnp.where(keep, here, above) for here, above in zip(turned + [zero], [zero] + turned)]
    size = 1
    while len(tiles) < most:
        move = jnp.broadcast_to((shift & (8 * size)) != 0, (8, LANE))
        still = tiles + [zero] * size
        moved = [zero] * size + tiles
        tiles = [jnp.where(move, moved[i], still[i]) for i in range(min(len(still), most))]
        size *= 2
    return jnp.concatenate(tiles + [zero] * (-most % 2), axis=0)


def indexing_kernel(begin, coarse, index_sizes, shift_ref, *rest):
    ids_ref, channel_ref, taps_ref, table_ref, u_ref, label_ref, slab_ref, wave = rest[-8:]
    index_kernel(*index_sizes, coarse, ids_ref, channel_ref, shift_ref, label_ref, slab_ref)
    template_kernel(begin, coarse, shift_ref, taps_ref, table_ref, u_ref, wave)


def template_kernel(begin, coarse, shift_ref, *rest):
    taps_ref, table_ref, u_ref, wave = rest[-4:]
    count, _, templates = taps_ref.shape
    most = (TL + coarse) // 16

    def halves_of(index):
        halves = [[], []]
        for j in range(index * GROUP, (index + 1) * GROUP):
            wave[...] = taps_ref[j].astype(F32)
            even, odd = wave[pl.ds(0, TL // 2, stride=2), :], wave[pl.ds(1, TL // 2, stride=2), :]
            shift = shift_ref[begin + j : begin + j + 1, :] % coarse
            swap = jnp.broadcast_to((shift & 1) != 0, even.shape)
            halves[0].append(delayed(jnp.where(swap, odd, even), (shift + 1) >> 1, most))
            halves[1].append(delayed(jnp.where(swap, even, odd), shift >> 1, most))
        return [jnp.concatenate([jnp.transpose(h.astype(BF16)) for h in half], axis=0) for half in halves]

    for index in range(count // GROUP):
        halves = halves_of(index)
        for q in range(4):
            sums = [jnp.dot(halves[p], table_ref[p, :, columns_of(q)], preferred_element_type=F32) for p in range(2)]
            for column, value in butterfly(q, *sums):
                for j in range(GROUP):
                    for g in range(templates // 8):
                        at = (g * 8 * count + index * GROUP + j) * PITCH + column
                        part = value[j * templates + g * 8 : j * templates + (g + 1) * 8]
                        u_ref[pl.ds(at, 8, stride=count * PITCH), :] = part


def index_kernel(slots, versions, coarse, ids_ref, channel_ref, shift_ref, label_ref, slab_ref):
    tmpl_count, width = label_ref.shape
    for t in range(tmpl_count):
        high, low = column_ids(ids_ref[...], t, tmpl_count, slots)
        digits = jnp.concatenate([high, low, jnp.zeros((14, high.shape[1]), F32)], axis=0).astype(BF16)
        pick = picks(high, low, width)
        row = lax.dot_general(digits, pick, (((1,), (1,)), ((), ())), preferred_element_type=F32)
        label_ref[t : t + 1, :] = (row[0:1] * 64.0 + row[1:2]).astype(jnp.int32) - 1
    slab_ref[0:CH, :] = channel_ref[...] * versions + shift_ref[...] // coarse
    slab_ref[CH:, :] = jnp.zeros((slab_ref.shape[0] - CH, slab_ref.shape[1]), jnp.int32)


def stack_kernel(live, versions, counts, in_main, slab_ref, label_ref, inverse_hbm, phase_ref, *rest):
    u_refs, pieces = rest[: len(counts)], rest[len(counts) : -8]
    out_ref, inverse, flat, slabs, z, packed, held, sems = rest[-8:]
    templates = out_ref.shape[0]
    table_copy = pltpu.make_async_copy(inverse_hbm, inverse, sems.at[0])
    table_copy.start()
    rows = held.shape[0]
    tmpl = lax.axis_index("tmpl")
    flat[rows * PITCH :, :] = jnp.zeros((8, LANE), F32)
    turns = [(phase_ref[a, 0:8], phase_ref[a, 8:16]) for a in range(1, versions)]
    fetches = [pltpu.make_async_copy(pieces[d], held, sems.at[1]) for d in in_main]
    fetches[0].start()
    for d in [d for d in range(len(pieces)) if d not in in_main] + list(in_main):
        piece = pieces[d]
        if d in in_main:
            which = in_main.index(d)
            if which:
                fetches[which].start()
            fetches[which].wait()
            piece = held
        for g in range(rows // 16):
            for column in range(2 * TILES):
                value = piece[g * 16 : (g + 1) * 16, column * LANE : (column + 1) * LANE].astype(F32)
                for h in range(2):
                    flat[pl.ds((2 * g + h) * 8 * PITCH + column, 8, stride=PITCH), :] = value[h * 8 : (h + 1) * 8]
        for r in range(live):
            label = label_ref[tmpl ^ d, r] * versions
            x_cos = flat[r * PITCH : r * PITCH + 8]
            x_sin = flat[r * PITCH + TILES : r * PITCH + TILES + 8]
            slabs[label, 0:8] = x_cos
            slabs[label, 8:16] = x_sin
            for a, (cosine, sine) in enumerate(turns):
                slabs[label + a + 1, 0:8] = x_cos * cosine + x_sin * sine
                slabs[label + a + 1, 8:16] = x_sin * cosine - x_cos * sine

    step = 4

    def several(i, carry):
        for q in range(step):
            k = i * step + q
            real, imag = [None, None], [None, None]
            j = 0
            for u_ref, count in zip(u_refs, counts):
                for own in range(count):
                    c = slab_ref[i * step + (j * templates + q)]
                    at = i * (step * count * PITCH) + (q * count + own) * PITCH
                    u_cos = u_ref[pl.ds(at, 8), :]
                    u_sin = u_ref[pl.ds(at + TILES, 8), :]
                    x_cos = slabs[c, 0:8]
                    x_sin = slabs[c, 8:16]
                    re = u_cos * x_cos + u_sin * x_sin
                    im = u_sin * x_cos - u_cos * x_sin
                    p = j % 2
                    real[p] = re if real[p] is None else real[p] + re
                    imag[p] = im if imag[p] is None else imag[p] + im
                    j += 1
            z[pl.ds(k, 8, stride=templates + 1), :] = real[0] + real[1]
            z[pl.ds(k + 8 * (templates + 1), 8, stride=templates + 1), :] = imag[0] + imag[1]
        return carry

    lax.fori_loop(0, templates // step, several, 0)

    first = lax.broadcasted_iota(jnp.int32, (templates, LANE), 1) == 0
    base = jnp.float32(CH * NS)
    for column in range(2 * TILES):
        row = column if column < TILES else column - TILES + 8
        weight = jnp.float32(2.0) / base
        if column % TILES == 0:
            weight = jnp.where(first, jnp.float32(1.0), jnp.float32(2.0)) / base
        value = z[row * (templates + 1) : row * (templates + 1) + templates, :] * weight
        packed[:, column * LANE : (column + 1) * LANE] = value.astype(BF16)
    table_copy.wait()
    out_ref[...] = jnp.dot(packed[...], inverse[...], preferred_element_type=F32)


def full(space=pltpu.VMEM):
    return pl.BlockSpec(memory_space=space)


def in_hbm(array):
    return pltpu.with_memory_space_constraint(array, pltpu.HBM)


def on_device(raw, ids, fir, taps, channels, shifts):
    win_count = lax.axis_size("win")
    tmpl_count = lax.axis_size("tmpl")
    slots, raw_t = raw.shape
    templates = taps.shape[0]
    live = 3 * slots * win_count // 5
    rows = -(-live // 16) * 16
    chan_total = live * tmpl_count
    table = forward_tables()
    inverse = jnp.asarray(inverse_table())

    blocks = raw_t // (DEC * BLOCK)
    extra = (NS - WIN_DEV) // BLOCK
    mine = pl.pallas_call(
        spectra_kernel,
        out_shape=[jax.ShapeDtypeStruct((slots, NS), BF16)] * win_count,
        in_specs=[full(pltpu.HBM)] * 3,
        out_specs=[full()] * win_count,
        scratch_shapes=[
            pltpu.VMEM((slots, raw_t + SPAN - DEC * BLOCK), BF16),
            pltpu.VMEM((1, NTAP), BF16),
            pltpu.VMEM((2, NS // 2, NF), BF16),
            pltpu.VMEM(((blocks + extra) * slots, BLOCK), BF16),
            pltpu.VMEM((2, win_count * slots, NS // 2), BF16),
            pltpu.SemaphoreType.DMA((4,)),
        ],
        compiler_params=pltpu.CompilerParams(vmem_limit_bytes=24 * MIB),
        name="spectra",
    )(in_hbm(raw), in_hbm(fir[None, :]), in_hbm(jnp.asarray(table)))

    small = chan_total <= 1024
    versions, coarse = (3, 112) if small else (1, MOVE)
    waves = in_hbm(taps.transpose(1, 2, 0))
    reach = -(-(TL + coarse) // 32) * 16
    head = in_hbm(jnp.asarray(table[:, :reach]))
    counts = (9, 18, 3)
    label_width = -(-live // LANE) * LANE

    def template_spectra(n, *afters):
        count = counts[n]
        kernel = functools.partial(template_kernel, sum(counts[:n]), coarse)
        out_shape = jax.ShapeDtypeStruct((templates * count * PITCH + 8, LANE), F32)
        more, indices, out_specs = (), [], full()
        if n == 0:
            kernel = functools.partial(indexing_kernel, 0, coarse, (slots, versions))
            out_shape = [
                out_shape,
                pltpu.HBM((tmpl_count, label_width), jnp.int32),
                pltpu.HBM((32, templates), jnp.int32),
            ]
            more, out_specs = (ids[None, :], channels.T), [full()] * 3
        begin = sum(counts[:n])
        taps_block = pl.BlockSpec(
            (pl.Element(count), pl.Element(TL), pl.Element(templates)), lambda i, begin=begin: (begin, 0, 0)
        )
        return pl.pallas_call(
            kernel,
            out_shape=out_shape,
            grid=(1,),
            in_specs=[full()] + [full(pl.ANY)] * len(afters) + [full()] * len(more) + [taps_block, full()],
            out_specs=out_specs,
            scratch_shapes=[pltpu.VMEM((TL, LANE), F32)],
            compiler_params=pltpu.CompilerParams(vmem_limit_bytes=(12 if small else 40) * MIB),
            name="templates",
        )(shifts.T, *afters, *more, waves, head)

    parts = {0: mine[0]}
    near = [d for d in (1, 2) if d < win_count]
    far = [d for d in range(win_count - 1, 0, -1) if d not in near]
    for d in near + far:
        parts[d] = lax.ppermute(mine[d], "win", [(i, i ^ d) for i in range(win_count)])
    early, labels, slab_index = template_spectra(0, *[parts[d] for d in near])
    parts, early, labels, slab_index = lax.optimization_barrier((parts, early, labels, slab_index))
    parts = [parts[d] for d in range(win_count)]

    packed_rows = pl.pallas_call(
        compact_kernel,
        out_shape=jax.ShapeDtypeStruct((rows, NS), BF16),
        in_specs=[full()] * (1 + win_count),
        out_specs=full(),
        scratch_shapes=[pltpu.VMEM((win_count * slots, NS), BF16)],
        compiler_params=pltpu.CompilerParams(vmem_limit_bytes=24 * MIB),
        name="compact",
    )(ids[None, :], *parts)

    late = template_spectra(1, packed_rows)
    held = {0: packed_rows}
    bit = tmpl_count // 2
    while bit:
        for d in list(held):
            source = held[d]
            if d and bit == 1:
                source, late = lax.optimization_barrier((source, late))
            held[d | bit] = lax.ppermute(source, "tmpl", [(i, i ^ bit) for i in range(tmpl_count)])
        bit //= 2
    last = template_spectra(2, late)
    pieces = [held[d] for d in range(tmpl_count)]

    in_main = (0,) if small else tuple(range(tmpl_count))
    places = [pltpu.HBM if d in in_main else pltpu.VMEM for d in range(tmpl_count)]
    return pl.pallas_call(
        functools.partial(stack_kernel, live, versions, counts, in_main),
        out_shape=jax.ShapeDtypeStruct((templates, WIN_DEV), F32),
        in_specs=[full(pltpu.SMEM)] * 2
        + [full(pltpu.HBM), full()]
        + [full()] * len(counts)
        + [full(space) for space in places],
        out_specs=full(),
        scratch_shapes=[
            pltpu.VMEM((2 * NF, WIN_DEV), BF16),
            pltpu.VMEM((rows * PITCH + 8, LANE), F32),
            pltpu.VMEM((chan_total * versions, 16, LANE), F32),
            pltpu.VMEM((16 * (templates + 1), LANE), F32),
            pltpu.VMEM((templates, NS), BF16),
            pltpu.VMEM((rows, NS), BF16),
            pltpu.SemaphoreType.DMA((2,)),
        ],
        compiler_params=pltpu.CompilerParams(vmem_limit_bytes=(19 if small else 58) * MIB),
        name="stacks",
    )(
        in_hbm(slab_index.reshape(-1)),
        in_hbm(labels),
        in_hbm(inverse),
        jnp.asarray(phase_table(versions, coarse)),
        early,
        late,
        last,
        *[in_hbm(piece) if d in in_main else piece for d, piece in enumerate(pieces)],
    )


def solution(mesh):
    return jax.shard_map(
        on_device,
        mesh=mesh,
        in_specs=(
            P(("win", "tmpl"), None),
            P(),
            P(),
            P("tmpl", None, None),
            P("tmpl", None),
            P("tmpl", None),
        ),
        out_specs=P("tmpl", "win"),
        check_vma=False,
    )
```

```python
import functools
import math

import jax
import jax.numpy as jnp
import ml_dtypes
import numpy as np
from jax import lax
from jax.experimental import pallas as pl
from jax.experimental.pallas import tpu as pltpu
from jax.sharding import PartitionSpec as P

WIN_DEV = 1024
TL = 400
CH = 30
DEC = 2
NTAP = 64
MOVE = 256
NS = 1792
NF = 896
LANE = 128
TILES = NF // LANE
BLOCK = 256
SPAN = 640
PITCH = 2 * TILES
GROUP = 3
MIB = 2**20
BF16 = jnp.bfloat16
F32 = jnp.float32


def angles(rows, columns):
    step = np.float32(2.0 * math.pi / NS)
    turns = np.arange(rows)[:, None] * np.arange(columns)[None, :] % NS
    return (turns.astype(np.float32) * step).astype(np.float64)


def order():
    low = np.arange(3 * LANE)
    high = NF - low
    high[0] = NF // 2
    rest = np.arange(3 * LANE, NF // 2)
    return np.concatenate([low, high, rest, NF - rest])


def forward_tables():
    angle = angles(NS, NF)
    cosine, sine = np.cos(angle), np.sin(angle)
    half = NF // 2
    columns = []
    for begin in range(0, half, LANE):
        end = min(begin + LANE, half)
        columns += [cosine[:, begin:end], sine[:, begin:end]]
    table = np.concatenate(columns, axis=1)
    even, odd = table[0::2].copy(), table[1::2].copy()
    even[:, LANE] = cosine[0::2, half]
    odd[:, LANE] = sine[1::2, half]
    return np.stack([even, odd]).astype(ml_dtypes.bfloat16)


def inverse_table():
    angle = angles(NF, WIN_DEV)[order()]
    return np.concatenate([np.cos(angle), -np.sin(angle)], axis=0).astype(ml_dtypes.bfloat16)


def phase_table(versions, coarse):
    angle = angles(versions * coarse, NF)[::coarse, order()]
    slab = np.zeros((versions, 16, LANE), np.float32)
    slab[:, :TILES] = np.cos(angle).reshape(versions, TILES, LANE)
    slab[:, 8 : 8 + TILES] = np.sin(angle).reshape(versions, TILES, LANE)
    return slab


def tile_of(array, column):
    return array[:, column * LANE : (column + 1) * LANE]


def butterfly(q, even, odd):
    lane = lax.broadcasted_iota(jnp.int32, (even.shape[0], LANE), 1)
    if q == 3:
        low, gap = even + odd, even - odd
        left = lane < LANE // 2
        yield 6, jnp.where(left, low, pltpu.roll(gap, LANE // 2, 1))
        yield 13, jnp.where(left, pltpu.roll(low, LANE // 2, 1), -gap)
        return
    low_cos, low_sin = tile_of(even, 0) + tile_of(odd, 0), tile_of(even, 1) + tile_of(odd, 1)
    high_cos, high_sin = tile_of(even, 0) - tile_of(odd, 0), tile_of(odd, 1) - tile_of(even, 1)
    if q == 0:
        low_sin = jnp.where(lane == 0, 0.0, low_sin)
        high_cos = jnp.where(lane == 0, tile_of(even, 1), high_cos)
        high_sin = jnp.where(lane == 0, tile_of(odd, 1), high_sin)
    yield q, low_cos
    yield 7 + q, low_sin
    yield 3 + q, high_cos
    yield 10 + q, high_sin


def columns_of(q):
    return slice(2 * q * LANE, min(2 * (q + 1) * LANE, NF))


def spectra_kernel(raw_hbm, fir_hbm, table_hbm, *rest):
    win_count = len(rest) - 6
    outs = rest[:win_count]
    raw, fir, table, filt, tile, sems = rest[win_count:]
    win = lax.axis_index("win")
    slots, raw_t = raw_hbm.shape
    length = DEC * BLOCK
    blocks = raw_t // length
    raw_copy = pltpu.make_async_copy(raw_hbm, raw.at[:, 0:raw_t], sems.at[0])
    raw_copy.start()
    fir_copy = pltpu.make_async_copy(fir_hbm, fir, sems.at[1])
    fir_copy.start()
    loads = [pltpu.make_async_copy(table_hbm.at[p], table.at[p], sems.at[2 + p]) for p in range(2)]
    for load in loads:
        load.start()
    raw[:, raw_t:] = jnp.zeros((slots, SPAN - length), BF16)
    fir_copy.wait()
    taps = jnp.concatenate([fir[...].astype(F32), jnp.zeros((1, SPAN - NTAP), F32)], axis=1)
    spread = jnp.broadcast_to(taps, (BLOCK // 2, SPAN))
    even = pltpu.roll(spread, 0, 1, stride=2 * DEC, stride_axis=0)
    odd = pltpu.roll(spread, DEC, 1, stride=2 * DEC, stride_axis=0)
    band = jnp.concatenate([even, odd], axis=0).astype(BF16)
    raw_copy.wait()
    segments = jnp.concatenate([raw[:, b * length : b * length + SPAN] for b in range(blocks)], axis=0)
    result = lax.dot_general(segments, band, (((1,), (1,)), ((), ())), preferred_element_type=F32)
    filt[0 : blocks * slots] = result.astype(BF16)
    per_win = WIN_DEV // BLOCK
    per_tile = NS // BLOCK
    filt[blocks * slots :] = jnp.zeros(((per_tile - per_win) * slots, BLOCK), BF16)
    for d in range(win_count):
        first = (win ^ d) * per_win
        for m in range(per_tile):
            start = pl.multiple_of((first + m) * slots, slots)
            block = filt[pl.ds(start, slots), :]
            for p in range(2):
                tile[p, d * slots : (d + 1) * slots, m * LANE : (m + 1) * LANE] = tile_of(block, p)
    values = tile[...].astype(F32)
    scale = lax.rsqrt(jnp.sum(jnp.sum(values * values, axis=2, keepdims=True), axis=0) / NS + 1e-05)
    for load in loads:
        load.wait()
    for q in range(4):
        sums = [jnp.dot(tile[p], table[p, :, columns_of(q)], preferred_element_type=F32) for p in range(2)]
        for column, value in butterfly(q, *sums):
            value = (value * scale).astype(BF16)
            for d in range(win_count):
                outs[d][:, column * LANE : (column + 1) * LANE] = value[d * slots : (d + 1) * slots]


def column_ids(ids, tmpl, tmpl_count, slots):
    total = ids.shape[1]
    count = total // tmpl_count
    source = lax.broadcasted_iota(jnp.int32, (total, count), 0)
    target = lax.broadcasted_iota(jnp.int32, (total, count), 1)
    wanted = (target // slots * tmpl_count + tmpl) * slots + target % slots
    pick = jnp.where(source == wanted, 1.0, 0.0).astype(BF16)
    digits = jnp.concatenate([(ids + 1) // 64, (ids + 1) % 64], axis=0).astype(F32)
    digits = jnp.concatenate([digits, jnp.zeros((14, total), F32)], axis=0).astype(BF16)
    found = jnp.dot(digits, pick, preferred_element_type=F32)
    return found[0:1], found[1:2]


def picks(high, low, rows):
    count = high.shape[1]
    live = high + low > 0.0
    above = lax.broadcasted_iota(jnp.int32, (count, count), 0) < lax.broadcasted_iota(
        jnp.int32, (count, count), 1
    )
    marks = jnp.broadcast_to(jnp.where(live, 1.0, 0.0), (16, count)).astype(BF16)
    rank = jnp.dot(marks, jnp.where(above, 1.0, 0.0).astype(BF16), preferred_element_type=F32)
    rank = jnp.where(live, rank[0:1], -1.0)
    wanted = lax.broadcasted_iota(jnp.int32, (rows, count), 0).astype(F32)
    return jnp.where(wanted == rank, 1.0, 0.0).astype(BF16)


def compact_kernel(ids_ref, *rest):
    blocks, out_ref, data = rest[:-2], rest[-2], rest[-1]
    slots = blocks[0].shape[0]
    win = lax.axis_index("win")
    high, low = column_ids(ids_ref[...], lax.axis_index("tmpl"), lax.axis_size("tmpl"), slots)
    pick = picks(high, low, out_ref.shape[0])
    for d, block in enumerate(blocks):
        start = pl.multiple_of((win ^ d) * slots, slots)
        data[pl.ds(start, slots), :] = block[...]
    out_ref[...] = jnp.dot(pick, data[...], preferred_element_type=F32).astype(BF16)


def delayed(wave, shift, most):
    row = lax.broadcasted_iota(jnp.int32, (8, LANE), 0)
    fine = jnp.broadcast_to(shift & 7, (8, LANE))
    keep = row >= fine
    source = (row - fine) & 7
    zero = jnp.zeros((8, LANE), F32)
    turned = [jnp.take_along_axis(wave[i : i + 8], source, axis=0) for i in range(0, wave.shape[0], 8)]
    tiles = [jnp.where(keep, here, above) for here, above in zip(turned + [zero], [zero] + turned)]
    size = 1
    while len(tiles) < most:
        move = jnp.broadcast_to((shift & (8 * size)) != 0, (8, LANE))
        still = tiles + [zero] * size
        moved = [zero] * size + tiles
        tiles = [jnp.where(move, moved[i], still[i]) for i in range(min(len(still), most))]
        size *= 2
    return jnp.concatenate(tiles + [zero] * (-most % 2), axis=0)


def indexing_kernel(begin, coarse, index_sizes, shift_ref, *rest):
    ids_ref, channel_ref, taps_ref, table_ref, u_ref, label_ref, slab_ref, wave = rest[-8:]
    index_kernel(*index_sizes, coarse, ids_ref, channel_ref, shift_ref, label_ref, slab_ref)
    template_kernel(begin, coarse, shift_ref, taps_ref, table_ref, u_ref, wave)


def template_kernel(begin, coarse, shift_ref, *rest):
    taps_ref, table_ref, u_ref, wave = rest[-4:]
    count, _, templates = taps_ref.shape
    most = (TL + coarse) // 16

    def halves_of(index):
        halves = [[], []]
        for j in range(index * GROUP, (index + 1) * GROUP):
            wave[...] = taps_ref[j].astype(F32)
            even, odd = wave[pl.ds(0, TL // 2, stride=2), :], wave[pl.ds(1, TL // 2, stride=2), :]
            shift = shift_ref[begin + j : begin + j + 1, :] % coarse
            swap = jnp.broadcast_to((shift & 1) != 0, even.shape)
            halves[0].append(delayed(jnp.where(swap, odd, even), (shift + 1) >> 1, most))
            halves[1].append(delayed(jnp.where(swap, even, odd), shift >> 1, most))
        return [jnp.concatenate([jnp.transpose(h.astype(BF16)) for h in half], axis=0) for half in halves]

    for index in range(count // GROUP):
        halves = halves_of(index)
        for q in range(4):
            sums = [jnp.dot(halves[p], table_ref[p, :, columns_of(q)], preferred_element_type=F32) for p in range(2)]
            for column, value in butterfly(q, *sums):
                for j in range(GROUP):
                    for g in range(templates // 8):
                        at = (g * 8 * count + index * GROUP + j) * PITCH + column
                        part = value[j * templates + g * 8 : j * templates + (g + 1) * 8]
                        u_ref[pl.ds(at, 8, stride=count * PITCH), :] = part


def index_kernel(slots, versions, coarse, ids_ref, channel_ref, shift_ref, label_ref, slab_ref):
    tmpl_count, width = label_ref.shape
    for t in range(tmpl_count):
        high, low = column_ids(ids_ref[...], t, tmpl_count, slots)
        digits = jnp.concatenate([high, low, jnp.zeros((14, high.shape[1]), F32)], axis=0).astype(BF16)
        pick = picks(high, low, width)
        row = lax.dot_general(digits, pick, (((1,), (1,)), ((), ())), preferred_element_type=F32)
        label_ref[t : t + 1, :] = (row[0:1] * 64.0 + row[1:2]).astype(jnp.int32) - 1
    slab_ref[0:CH, :] = channel_ref[...] * versions + shift_ref[...] // coarse
    slab_ref[CH:, :] = jnp.zeros((slab_ref.shape[0] - CH, slab_ref.shape[1]), jnp.int32)


def stack_kernel(live, versions, counts, in_main, slab_hbm, label_hbm, inverse_hbm, phase_ref, *rest):
    u_refs, pieces = rest[: len(counts)], rest[len(counts) : -11]
    out_hbm, inverse, flat, slabs, z, packed, held, result, slab_ref, label_ref, sems = rest[-11:]
    templates = result.shape[0]
    label_copy = pltpu.make_async_copy(label_hbm, label_ref, sems.at[2])
    label_copy.start()
    slab_copy = pltpu.make_async_copy(slab_hbm, slab_ref, sems.at[3])
    slab_copy.start()
    table_copy = pltpu.make_async_copy(inverse_hbm, inverse, sems.at[0])
    table_copy.start()
    rows = held.shape[0]
    tmpl = lax.axis_index("tmpl")
    flat[rows * PITCH :, :] = jnp.zeros((8, LANE), F32)
    turns = [(phase_ref[a, 0:8], phase_ref[a, 8:16]) for a in range(1, versions)]
    fetches = [pltpu.make_async_copy(pieces[d], held, sems.at[1]) for d in in_main]
    fetches[0].start()
    scattered = False
    for d in [d for d in range(len(pieces)) if d not in in_main] + list(in_main):
        piece = pieces[d]
        if d in in_main:
            which = in_main.index(d)
            if which:
                fetches[which].start()
            fetches[which].wait()
            piece = held
        for g in range(rows // 16):
            for column in range(2 * TILES):
                value = piece[g * 16 : (g + 1) * 16, column * LANE : (column + 1) * LANE].astype(F32)
                for h in range(2):
                    flat[pl.ds((2 * g + h) * 8 * PITCH + column, 8, stride=PITCH), :] = value[h * 8 : (h + 1) * 8]
        if not scattered:
            label_copy.wait()
        scattered = True
        for r in range(live):
            label = label_ref[tmpl ^ d, r] * versions
            x_cos = flat[r * PITCH : r * PITCH + 8]
            x_sin = flat[r * PITCH + TILES : r * PITCH + TILES + 8]
            slabs[label, 0:8] = x_cos
            slabs[label, 8:16] = x_sin
            for a, (cosine, sine) in enumerate(turns):
                slabs[label + a + 1, 0:8] = x_cos * cosine + x_sin * sine
                slabs[label + a + 1, 8:16] = x_sin * cosine - x_cos * sine

    step = 4

    def several(i, carry):
        for q in range(step):
            k = i * step + q
            real, imag = [None, None], [None, None]
            j = 0
            for u_ref, count in zip(u_refs, counts):
                for own in range(count):
                    c = slab_ref[i * step + (j * templates + q)]
                    at = i * (step * count * PITCH) + (q * count + own) * PITCH
                    u_cos = u_ref[pl.ds(at, 8), :]
                    u_sin = u_ref[pl.ds(at + TILES, 8), :]
                    x_cos = slabs[c, 0:8]
                    x_sin = slabs[c, 8:16]
                    re = u_cos * x_cos + u_sin * x_sin
                    im = u_sin * x_cos - u_cos * x_sin
                    p = j % 2
                    real[p] = re if real[p] is None else real[p] + re
                    imag[p] = im if imag[p] is None else imag[p] + im
                    j += 1
            z[pl.ds(k, 8, stride=templates + 1), :] = real[0] + real[1]
            z[pl.ds(k + 8 * (templates + 1), 8, stride=templates + 1), :] = imag[0] + imag[1]
        return carry

    slab_copy.wait()
    lax.fori_loop(0, templates // step, several, 0)

    first = lax.broadcasted_iota(jnp.int32, (templates, LANE), 1) == 0
    base = jnp.float32(CH * NS)
    for column in range(2 * TILES):
        row = column if column < TILES else column - TILES + 8
        weight = jnp.float32(2.0) / base
        if column % TILES == 0:
            weight = jnp.where(first, jnp.float32(1.0), jnp.float32(2.0)) / base
        value = z[row * (templates + 1) : row * (templates + 1) + templates, :] * weight
        packed[:, column * LANE : (column + 1) * LANE] = value.astype(BF16)
    table_copy.wait()
    stores = []
    width = 2 * LANE
    for n in range(WIN_DEV // width):
        part = slice(n * width, (n + 1) * width)
        result[:, part] = jnp.dot(packed[...], inverse[:, part], preferred_element_type=F32)
        stores.append(pltpu.make_async_copy(result.at[:, part], out_hbm.at[:, part], sems.at[4 + n]))
        stores[-1].start()
    for store in stores:
        store.wait()


def full(space=pltpu.VMEM):
    return pl.BlockSpec(memory_space=space)


def in_hbm(array):
    return pltpu.with_memory_space_constraint(array, pltpu.HBM)


def on_device(raw, ids, fir, taps, channels, shifts):
    win_count = lax.axis_size("win")
    tmpl_count = lax.axis_size("tmpl")
    slots, raw_t = raw.shape
    templates = taps.shape[0]
    live = 3 * slots * win_count // 5
    rows = -(-live // 16) * 16
    chan_total = live * tmpl_count
    table = forward_tables()
    inverse = jnp.asarray(inverse_table())

    blocks = raw_t // (DEC * BLOCK)
    extra = (NS - WIN_DEV) // BLOCK
    mine = pl.pallas_call(
        spectra_kernel,
        out_shape=[jax.ShapeDtypeStruct((slots, NS), BF16)] * win_count,
        in_specs=[full(pltpu.HBM)] * 3,
        out_specs=[full()] * win_count,
        scratch_shapes=[
            pltpu.VMEM((slots, raw_t + SPAN - DEC * BLOCK), BF16),
            pltpu.VMEM((1, NTAP), BF16),
            pltpu.VMEM((2, NS // 2, NF), BF16),
            pltpu.VMEM(((blocks + extra) * slots, BLOCK), BF16),
            pltpu.VMEM((2, win_count * slots, NS // 2), BF16),
            pltpu.SemaphoreType.DMA((4,)),
        ],
        compiler_params=pltpu.CompilerParams(vmem_limit_bytes=24 * MIB),
        name="spectra",
    )(in_hbm(raw), in_hbm(fir[None, :]), in_hbm(jnp.asarray(table)))

    small = chan_total <= 1024
    versions, coarse = (3, 112) if small else (1, MOVE)
    waves = in_hbm(taps.transpose(1, 2, 0))
    reach = -(-(TL + coarse) // 32) * 16
    head = in_hbm(jnp.asarray(table[:, :reach]))
    counts = (9, 18, 3)
    label_width = -(-live // LANE) * LANE

    def template_spectra(n, *afters):
        count = counts[n]
        kernel = functools.partial(template_kernel, sum(counts[:n]), coarse)
        out_shape = jax.ShapeDtypeStruct((templates * count * PITCH + 8, LANE), F32)
        more, indices, out_specs = (), [], full()
        if n == 0:
            kernel = functools.partial(indexing_kernel, 0, coarse, (slots, versions))
            out_shape = [
                out_shape,
                pltpu.HBM((tmpl_count, label_width), jnp.int32),
                pltpu.HBM((32, templates), jnp.int32),
            ]
            more, out_specs = (ids[None, :], channels.T), [full()] * 3
        begin = sum(counts[:n])
        taps_block = pl.BlockSpec(
            (pl.Element(count), pl.Element(TL), pl.Element(templates)), lambda i, begin=begin: (begin, 0, 0)
        )
        return pl.pallas_call(
            kernel,
            out_shape=out_shape,
            grid=(1,),
            in_specs=[full()] + [full(pl.ANY)] * len(afters) + [full()] * len(more) + [taps_block, full()],
            out_specs=out_specs,
            scratch_shapes=[pltpu.VMEM((TL, LANE), F32)],
            compiler_params=pltpu.CompilerParams(vmem_limit_bytes=(12 if small else 40) * MIB),
            name="templates",
        )(shifts.T, *afters, *more, waves, head)

    parts = {0: mine[0]}
    near = [d for d in (1, 2) if d < win_count]
    far = [d for d in range(win_count - 1, 0, -1) if d not in near]
    for d in near + far:
        parts[d] = lax.ppermute(mine[d], "win", [(i, i ^ d) for i in range(win_count)])
    early, labels, slab_index = template_spectra(0, *[parts[d] for d in near])
    parts, early, labels, slab_index = lax.optimization_barrier((parts, early, labels, slab_index))
    parts = [parts[d] for d in range(win_count)]

    packed_rows = pl.pallas_call(
        compact_kernel,
        out_shape=jax.ShapeDtypeStruct((rows, NS), BF16),
        in_specs=[full()] * (1 + win_count),
        out_specs=full(),
        scratch_shapes=[pltpu.VMEM((win_count * slots, NS), BF16)],
        compiler_params=pltpu.CompilerParams(vmem_limit_bytes=24 * MIB),
        name="compact",
    )(ids[None, :], *parts)

    late = template_spectra(1, packed_rows)
    held = {0: packed_rows}
    bit = tmpl_count // 2
    while bit:
        for d in list(held):
            source = held[d]
            if d and bit == 1:
                source, late = lax.optimization_barrier((source, late))
            held[d | bit] = lax.ppermute(source, "tmpl", [(i, i ^ bit) for i in range(tmpl_count)])
        bit //= 2
    last = template_spectra(2, late)
    pieces = [held[d] for d in range(tmpl_count)]

    in_main = (0,) if small else tuple(range(tmpl_count))
    places = [pltpu.HBM if d in in_main else pltpu.VMEM for d in range(tmpl_count)]
    return pl.pallas_call(
        functools.partial(stack_kernel, live, versions, counts, in_main),
        out_shape=jax.ShapeDtypeStruct((templates, WIN_DEV), F32),
        in_specs=[full(pltpu.HBM)] * 3
        + [full()]
        + [full()] * len(counts)
        + [full(space) for space in places],
        out_specs=full(pltpu.HBM),
        scratch_shapes=[
            pltpu.VMEM((2 * NF, WIN_DEV), BF16),
            pltpu.VMEM((rows * PITCH + 8, LANE), F32),
            pltpu.VMEM((chan_total * versions, 16, LANE), F32),
            pltpu.VMEM((16 * (templates + 1), LANE), F32),
            pltpu.VMEM((templates, NS), BF16),
            pltpu.VMEM((rows, NS), BF16),
            pltpu.VMEM((templates, WIN_DEV), F32),
            pltpu.SMEM((32 * templates,), jnp.int32),
            pltpu.SMEM((tmpl_count, label_width), jnp.int32),
            pltpu.SemaphoreType.DMA((8,)),
        ],
        compiler_params=pltpu.CompilerParams(vmem_limit_bytes=(19 if small else 58) * MIB),
        name="stacks",
    )(
        in_hbm(slab_index.reshape(-1)),
        in_hbm(labels),
        in_hbm(inverse),
        jnp.asarray(phase_table(versions, coarse)),
        early,
        late,
        last,
        *[in_hbm(piece) if d in in_main else piece for d, piece in enumerate(pieces)],
    )


def solution(mesh):
    return jax.shard_map(
        on_device,
        mesh=mesh,
        in_specs=(
            P(("win", "tmpl"), None),
            P(),
            P(),
            P("tmpl", None, None),
            P("tmpl", None),
            P("tmpl", None),
        ),
        out_specs=P("tmpl", "win"),
        check_vma=False,
    )
```
